32 devices in a mesh: chan: 16 (over z, y, x), tm: 2 (over core).
Axes of the slice: x: 2, y: 2, z: 4, core: 2. Of those that a mesh axis runs over, the one named last changes fastest.
Arguments:
- samples: bfloat16 [128, 524288], P('chan', 'tm'), may hold values from -8 to 8
- taps: float32 [16, 4096], replicated, may hold values from -0.0234375 to 0.0234375
- steering: float32 [8, 128], replicated, may hold values from -6 to 6
- interferer_ids: int32 [2048, 4], P(('chan', 'tm')), may hold values from 0 to 7, all different within a row
- ranks: int32 [2048], P(('chan', 'tm')), may hold values from 0 to 4
Outputs:
- covariance: float32 [2048, 2, 128, 128], P(('chan', 'tm'))
The draws below stay inside these ranges and needn't reach their ends.
Inputs may be any that keep to these rules, and one draw needn't show every extreme that they name: `interferer_ids`: the 4 entries of one channel's row name different directions.
All inputs are finite; a program needn't handle non-finite values.
Results may differ from the reference program's by a relative error of at most 0.00075.
Values may be sent and summed in bfloat16 or wider, within the bound.
No kernel may reach another device: no remote copies, remote signals or barrier semaphores. Data moves between devices by JAX's collectives and lax.ppermute only.
A program may use at most 128 MiB of HBM per device.

```python
import jax
import jax.numpy as jnp
from jax import lax

ARRAY_ELEMENTS = 128
KEPT_CHANNELS = 2048
TAPS = 16
JAMMER_BEARINGS = 8
RMAX = 4
L = 4096
FRAMES = 128


def mixing(key):
    sample_values = jax.random.normal(jax.random.fold_in(key, 11), (JAMMER_BEARINGS, ARRAY_ELEMENTS), jnp.float32)
    return jnp.clip(sample_values, -6.0, 6.0)


def draw_steering(key, part):
    return mixing(key)


def draw_samples(key, part):
    overall_length = FRAMES * L
    jitter_key = jax.random.fold_in(key, 23)
    source_key = jax.random.fold_in(key, 29)
    thermal_jitter = jax.random.normal(jitter_key, (ARRAY_ELEMENTS, overall_length), jnp.float32)
    strength = 0.5
    sources = jax.random.normal(source_key, (JAMMER_BEARINGS, overall_length), jnp.float32) * strength
    mixer = mixing(key)
    mixed = thermal_jitter
    for direction in range(JAMMER_BEARINGS):
        mixed = mixed + mixer[direction][:, None] * sources[direction][None, :]
    return jnp.clip(mixed, -8.0, 8.0).astype(jnp.bfloat16)


def place_ends(result, stream_key, smallest, largest):
    longest = result.shape.index(max(result.shape))
    spots = []
    for shift in (0, 1):
        where = [jax.random.randint(jax.random.fold_in(stream_key, axis), (), 0, length) for axis, length in enumerate(result.shape)]
        where[longest] = (where[longest] + shift) % result.shape[longest]
        spots.append(tuple(where))
    return result.at[spots[0]].set(smallest).at[spots[1]].set(largest)


def choose_distinct(key, rows, count, top, lift):
    sequence = jax.random.permutation(jax.random.fold_in(key, 1), count)
    boost = sequence
    for power in range(3):
        boost = boost * boost // count
    boost = boost * lift // count
    chance = jax.random.randint(jax.random.fold_in(key, 2), (rows, count), 0, 4096) + boost
    fixed_rows = jax.random.permutation(jax.random.fold_in(key, 3), rows)[jnp.arange(count) % rows]
    chance = jnp.where(jnp.arange(rows)[:, None] == fixed_rows[None, :], 1 << 14, chance)
    merit = chance * count + jnp.arange(count)
    return lax.top_k(merit.astype(jnp.int32), top)[1].astype(jnp.int32)


def normal_values(rng, dims, spread, limit, held_as=jnp.bfloat16):
    array = spread * jax.random.normal(rng, dims, jnp.float32)
    return jnp.clip(array, min=-limit, max=limit).astype(held_as)


def setup_inputs(seed: int = 0) -> dict:
    splits = jax.random.split(jax.random.key(seed), 6)
    samples = draw_samples(jax.random.fold_in(splits[5], 71), 0)
    taps = normal_values(splits[1], (TAPS, L), (TAPS * L) ** -0.5, 0.0234375, jnp.float32)
    steering = draw_steering(jax.random.fold_in(splits[5], 71), 0)
    interferer_ids = choose_distinct(splits[3], KEPT_CHANNELS, JAMMER_BEARINGS, RMAX, 0)
    ranks = place_ends(jax.random.randint(splits[4], (KEPT_CHANNELS,), 0, RMAX + 1), jax.random.fold_in(splits[4], 1), 0, RMAX).astype(jnp.int32)
    return dict(samples=samples, taps=taps, steering=steering, interferer_ids=interferer_ids, ranks=ranks)


epsilon = 1e-06
highest = lax.Precision.HIGHEST

def orthonormal(vectors):
    found = []
    for column in range(vectors.shape[1]):
        residue = vectors[:, column, :]
        for earlier in found:
            residue = residue - earlier * lax.optimization_barrier(jnp.sum(earlier * residue, axis=-1, keepdims=True))
        found.append(residue / jnp.sqrt(lax.optimization_barrier(jnp.sum(residue * residue, axis=-1, keepdims=True)) + epsilon))
    return jnp.stack(found, axis=1)

def project_out(gram, chosen, counted, steering, frame_total):
    slots = chosen.shape[1]
    live = (jnp.arange(slots, dtype=jnp.int32)[None, :] < counted[:, None]).astype(jnp.float32)
    vectors = steering[chosen] * live[:, :, None]
    basis = orthonormal(vectors)
    left = jnp.einsum('cra,csab->csrb', basis, gram, precision=highest)
    right = jnp.einsum('csab,crb->csar', gram, basis, precision=highest)
    core = jnp.einsum('csrb,ctb->csrt', left, basis, precision=highest)
    inner = jnp.einsum('csrt,ctb->csrb', core, basis, precision=highest)
    suppressed_output = gram - jnp.einsum('cra,csrb->csab', basis, left, precision=highest)
    suppressed_output = suppressed_output - jnp.einsum('csar,crb->csab', right, basis, precision=highest)
    suppressed_output = suppressed_output + jnp.einsum('cra,csrb->csab', basis, inner, precision=highest)
    return suppressed_output / frame_total

def reference(samples, taps, steering, interferer_ids, ranks):

    def channelize(signal):
        blocks = signal.astype(jnp.float32).reshape(FRAMES, L)
        padded = jnp.concatenate([jnp.zeros((TAPS - 1, L), jnp.float32), blocks], axis=0)
        filtered = jnp.zeros((FRAMES, L), jnp.float32)
        for tap_index in range(TAPS):
            filtered = filtered + taps[tap_index] * padded[tap_index:tap_index + FRAMES]
        spectrum = jnp.fft.rfft(filtered, axis=-1)[:, :KEPT_CHANNELS]
        return jnp.stack([jnp.real(spectrum), jnp.imag(spectrum)], axis=0).astype(jnp.bfloat16)
    spectra = lax.map(channelize, samples)
    width = 64

    def per_block(start):
        piece = lax.dynamic_slice_in_dim(spectra, start, width, axis=3).astype(jnp.float32)
        outer = jnp.einsum('arfc,bsfc->crasb', piece, piece, precision=highest)
        real_part = outer[:, 0, :, 0, :] + outer[:, 1, :, 1, :]
        imag_part = outer[:, 1, :, 0, :] - outer[:, 0, :, 1, :]
        gram = jnp.stack([real_part, imag_part], axis=1)
        chosen = lax.dynamic_slice_in_dim(interferer_ids, start, width, axis=0)
        counted = lax.dynamic_slice_in_dim(ranks, start, width, axis=0)
        return project_out(gram, chosen, counted, steering, FRAMES)
    starts = (jnp.arange(KEPT_CHANNELS // width) * width).astype(jnp.int32)
    suppressed_output = lax.map(per_block, starts)
    return suppressed_output.reshape(KEPT_CHANNELS, 2, ARRAY_ELEMENTS, ARRAY_ELEMENTS)
```

```python
import functools
import math

import jax
import jax.numpy as jnp
import ml_dtypes
import numpy as np
from jax import lax
from jax.experimental import pallas as pl
from jax.experimental.pallas import tpu as pltpu
from jax.sharding import PartitionSpec as P

lanes = 128
octet = 8
frame_block = 16
epsilon = 1e-06
highest = lax.Precision.HIGHEST
f32 = jnp.float32
bf16 = jnp.bfloat16
vmem_bytes = 56 * 1024 * 1024


def real_transform(x):
    size = len(x)
    if size == 2:
        return [(x[0] + x[1], None), (x[0] - x[1], None)]
    even = real_transform(x[0::2])
    odd = real_transform(x[1::2])
    half = size // 2
    bins = [None] * (half + 1)
    bins[0] = (even[0][0] + odd[0][0], None)
    bins[half] = (even[0][0] - odd[0][0], None)
    bins[half // 2] = (even[half // 2][0], -odd[half // 2][0])
    for k in range(1, half // 2):
        er, ei = even[k]
        o_r, oi = odd[k]
        c = math.cos(2 * math.pi * k / size)
        s = math.sin(2 * math.pi * k / size)
        if 4 * k == half:
            tr = (o_r + oi) * c
            ti = (oi - o_r) * c
        else:
            tr = o_r * c + oi * s
            ti = oi * c - o_r * s
        bins[k] = (er + tr, ei + ti)
        bins[half - k] = (er - tr, ti - ei)
    return bins


def split_two(x):
    high = x.astype(bf16)
    low = (x - high.astype(f32)).astype(bf16)
    return high, low


def split_three(x):
    high = x.astype(bf16).astype(f32)
    rest = x - high
    middle = rest.astype(bf16).astype(f32)
    return high, middle, rest - middle


def filter_kernel(length, before_ref, block_ref, taps_ref, *rest):
    high_ref, low_ref, filtered, sections = rest[-4:]
    tap_count = taps_ref.shape[0]
    radix = length // lanes

    @pl.loop(0, radix)
    def _(part):
        spot = pl.multiple_of(part * lanes, lanes)
        taps = [
            jnp.broadcast_to(taps_ref[pl.ds(t, 1), pl.ds(spot, lanes)], (octet, lanes))
            for t in range(tap_count)
        ]

        def sample(frame):
            ref = block_ref if frame >= 0 else before_ref
            place = pl.multiple_of(spot + frame % frame_block * length, lanes)
            return ref[:, pl.ds(place, lanes)].astype(f32)

        window = [sample(frame) for frame in range(1 - tap_count, 0)]
        for frame in range(frame_block):
            window.append(sample(frame))
            total = taps[0] * window[0]
            for t in range(1, tap_count):
                total = total + taps[t] * window[t]
            filtered[part, frame] = total
            window.pop(0)

    @pl.loop(0, frame_block)
    def _(frame):
        bins = real_transform([filtered[part, frame] for part in range(radix)])
        rows = pl.ds(frame, octet, stride=frame_block)
        sections[0, rows, :] = bins[0][0]
        sections[1, rows, :] = bins[radix // 2][0]
        for k in range(1, radix // 2):
            sections[2 * k, rows, :] = bins[k][0]
            sections[2 * k + 1, rows, :] = bins[k][1]

    def parts_of(group):
        shape = (octet, frame_block, lanes)
        real = sections[2 * group].reshape(shape)
        imag = sections[2 * group + 1].reshape(shape)
        return split_two(real), split_two(imag)

    reals, imags = parts_of(0)
    for ref, real, imag in zip((high_ref, low_ref), reals, imags):
        for turn in range(2):
            ref[0, :, turn, :, :lanes] = real
            ref[0, :, turn, :, lanes:] = imag

    @pl.loop(1, radix // 2)
    def _(group):
        reals, imags = parts_of(group)
        for ref, real, imag in zip((high_ref, low_ref), reals, imags):
            ref[group, :, 0, :, :lanes] = real
            ref[group, :, 0, :, lanes:] = imag
            ref[group, :, 1, :, :lanes] = imag
            ref[group, :, 1, :, lanes:] = -real


def filter_sections(before, samples, taps, first, steps, previous=None):
    length = taps.shape[1]
    frames = samples.shape[1] // length
    groups = length // lanes // 2
    width = frame_block * length
    shape = jax.ShapeDtypeStruct((groups, octet, 2, frames, 2 * lanes), bf16)
    block = pl.BlockSpec(
        (groups, octet, 2, frame_block, 2 * lanes), lambda i: (0, 0, 0, i + first, 0)
    )
    in_specs = [
        pl.BlockSpec((octet, width), lambda i: (0, i)),
        pl.BlockSpec((octet, width), lambda i: (0, i + first)),
        pl.BlockSpec(taps.shape, lambda i: (0, 0)),
    ]
    operands = [before, samples, taps]
    aliases = {}
    if previous is not None:
        in_specs += [pl.BlockSpec(memory_space=pl.ANY)] * 2
        operands += previous
        aliases = {3: 0, 4: 1}
    return pl.pallas_call(
        functools.partial(filter_kernel, length),
        grid=(steps,),
        in_specs=in_specs,
        out_specs=[block, block],
        out_shape=[shape, shape],
        scratch_shapes=[
            pltpu.VMEM((length // lanes, frame_block, octet, lanes), f32),
            pltpu.VMEM((length // lanes, frame_block * octet, lanes), f32),
        ],
        input_output_aliases=aliases,
        compiler_params=pltpu.CompilerParams(vmem_limit_bytes=vmem_bytes),
        cost_estimate=pl.CostEstimate(
            flops=steps * 80_000_000, bytes_accessed=steps * 6_000_000, transcendentals=0
        ),
        name="filter_sections",
    )(*operands)


def phase_tables(length):
    radix = length // lanes
    kept = lanes // 2
    q = np.arange(lanes)
    m = np.arange(kept)

    def angles(k):
        return 2 * np.pi * ((np.outer(k + radix * m, q)) % length) / length

    zero = np.zeros((kept, lanes))
    first, middle = angles(0), angles(radix // 2)
    tables = [np.block([[np.cos(first), zero], [zero, np.cos(middle)]])]
    for k in range(1, radix // 2):
        one, other = angles(k), angles(radix - k)
        tables.append(np.block([[np.cos(one), np.sin(one)], [np.cos(other), -np.sin(other)]]))
    tables.append(np.block([[-np.sin(first), zero], [zero, -np.sin(middle)]]))
    tables = np.stack(tables).astype(np.float32)
    high = tables.astype(ml_dtypes.bfloat16)
    low = (tables - high.astype(np.float32)).astype(ml_dtypes.bfloat16)
    return high, low


def contract_last(left, right):
    return lax.dot_general(left, right, (((1,), (1,)), ((), ())), preferred_element_type=f32)


def channel_kernel(
    with_zero, high_ref, low_ref, mh_ref, ml_ref, ih_ref, il_ref, out_ref, turned
):
    frames = high_ref.shape[3]
    kept = mh_ref.shape[1] // 2
    lane = lax.broadcasted_iota(jnp.int32, (1, lanes), 1)
    imaginary = lane >= frames

    def product(a, table_high, table_low):
        rows = (2 * lanes, 2 * lanes)
        high = high_ref[0, 2 * a : 2 * a + 2].reshape(rows)
        low = low_ref[0, 2 * a : 2 * a + 2].reshape(rows)
        total = contract_last(table_high, high) + contract_last(table_high, low)
        return total + contract_last(table_low, high)

    def body(zero):
        flip = jnp.where(imaginary, -1.0, 1.0)
        for a in range(octet // 2):
            total = product(a, mh_ref[0], ml_ref[0])
            if zero:
                other = product(a, ih_ref[0], il_ref[0])
            for side in range(2):
                piece = total[:, side * lanes : (side + 1) * lanes]
                if zero:
                    piece = jnp.where(imaginary, other[:, side * lanes : (side + 1) * lanes], piece)
                    lower = piece[kept:]
                else:
                    lower = piece[kept:] * flip
                turned[0, pl.ds(2 * a + side, kept, stride=octet), :] = piece[:kept]
                turned[1, pl.ds(2 * a + side, kept, stride=octet), :] = lower
        for half in range(2):
            out_ref[:, half] = turned[half].reshape(kept, octet, lanes).astype(bf16)

    if with_zero:
        step = pl.program_id(0)

        @pl.when(step == 0)
        def _():
            body(True)

        @pl.when(step != 0)
        def _():
            body(False)
    else:
        body(False)


def channels_of(sections, tables, first, count):
    high, low = sections
    groups, _, _, frames, _ = high.shape
    kept = tables[0].shape[1] // 2
    section = pl.BlockSpec((1, octet, 2, frames, 2 * lanes), lambda i: (i + first, 0, 0, 0, 0))
    table = pl.BlockSpec((1, 2 * kept, 2 * lanes), lambda i: (i + first, 0, 0))
    extra = pl.BlockSpec((1, 2 * kept, 2 * lanes), lambda i: (groups, 0, 0))
    return pl.pallas_call(
        functools.partial(channel_kernel, first == 0),
        grid=(count,),
        in_specs=[section, section, table, table, extra, extra],
        out_specs=pl.BlockSpec((kept, 2, octet, lanes), lambda i: (0, i, 0, 0)),
        out_shape=jax.ShapeDtypeStruct((kept, 2 * count, octet, lanes), bf16),
        scratch_shapes=[pltpu.VMEM((2, kept * octet, lanes), f32)],
        compiler_params=pltpu.CompilerParams(vmem_limit_bytes=vmem_bytes),
        cost_estimate=pl.CostEstimate(
            flops=count * 400_000_000, bytes_accessed=count * 1_500_000, transcendentals=0
        ),
        name="channels_of",
    )(high, low, *tables, *tables)


def covariance_kernel(place, scale, x_ref, q_ref, *rest):
    out_ref, ready, done = rest[-3:]
    step = pl.program_id(0)
    steps = pl.num_programs(0)
    slot = lax.rem(step, 2)
    octets, shards, count = x_ref.shape[:3]
    antennas = octets * octet
    half = lanes // 2
    sign = jnp.where(lax.broadcasted_iota(jnp.int32, (1, lanes), 1) < half, 1.0, -1.0)

    def copies(at, which):
        return [
            pltpu.make_async_copy(
                ready.at[which, j], out_ref.at[place(at * count + j)], done.at[which, j]
            )
            for j in range(count)
        ]

    @pl.when(step >= 2)
    def _():
        for copy in copies(step - 2, slot):
            copy.wait()

    for j in range(count):
        pieces = [x_ref[:, t, j].astype(f32).reshape(antennas, lanes) for t in range(shards)]
        x = jnp.concatenate(pieces, axis=1)
        q = q_ref[place(step * count + j)]
        qh, qm, ql = split_three(q)
        left = jnp.concatenate([qh, qm, ql, jnp.zeros_like(q)], axis=0).astype(bf16)
        z = jnp.dot(left, x.astype(bf16), preferred_element_type=f32)
        z = z[:octet] + z[octet : 2 * octet] + z[2 * octet : 3 * octet]
        zh, zm, zl = split_three(z)
        left = jnp.concatenate([qh, qh, qm, qm, qh, ql], axis=0).astype(bf16)
        right = jnp.concatenate([zh, zm, zh, zm, zl, zh], axis=0).astype(bf16)
        y = x - lax.dot_general(left, right, (((0,), (0,)), ((), ())), preferred_element_type=f32)
        high, low = split_two(y)

        def turned(v):
            v = v.astype(f32)
            parts = [
                pltpu.roll(v[:, t * lanes : (t + 1) * lanes], half, 1) * sign for t in range(shards)
            ]
            return jnp.concatenate(parts, axis=1).astype(bf16)

        both = contract_last(
            jnp.concatenate([high, turned(high)], axis=0), jnp.concatenate([high, low], axis=0)
        )
        rest_ = contract_last(jnp.concatenate([low, turned(low)], axis=0), high)
        total = (both[:, :antennas] + (both[:, antennas:] + rest_)) * scale
        ready[slot, j] = total.reshape(2, antennas, antennas)

    for copy in copies(step, slot):
        copy.start()

    @pl.when(step == steps - 1)
    def _():
        @pl.when(step >= 1)
        def _():
            for copy in copies(step - 1, 1 - slot):
                copy.wait()

        for copy in copies(step, slot):
            copy.wait()


def covariances(received, basis, place, frame_total, total, previous):
    octets, shards, channels = received.shape[:3]
    antennas = octets * octet
    count = math.gcd(channels, 4)
    in_specs = [
        pl.BlockSpec((octets, shards, count, octet, lanes), lambda i: (0, 0, i, 0, 0)),
        pl.BlockSpec(basis.shape, lambda i: (0, 0, 0)),
    ]
    operands = [received, basis]
    aliases = {}
    if previous is not None:
        in_specs.append(pl.BlockSpec(memory_space=pl.ANY))
        operands.append(previous)
        aliases = {2: 0}
    return pl.pallas_call(
        functools.partial(covariance_kernel, place, 1.0 / frame_total),
        grid=(channels // count,),
        in_specs=in_specs,
        out_specs=pl.BlockSpec(memory_space=pl.ANY),
        out_shape=jax.ShapeDtypeStruct((total, 2, antennas, antennas), f32),
        scratch_shapes=[
            pltpu.VMEM((2, count, 2, antennas, antennas), f32),
            pltpu.SemaphoreType.DMA((2, count)),
        ],
        input_output_aliases=aliases,
        compiler_params=pltpu.CompilerParams(vmem_limit_bytes=vmem_bytes),
        cost_estimate=pl.CostEstimate(
            flops=channels * 60_000_000, bytes_accessed=channels * 250_000, transcendentals=0
        ),
        name="covariances",
    )(*operands)


def orthonormal(vectors):
    found = []
    for column in range(vectors.shape[1]):
        residue = vectors[:, column, :]
        for earlier in found:
            residue = residue - earlier * jnp.sum(earlier * residue, axis=-1, keepdims=True)
        found.append(
            residue / jnp.sqrt(jnp.sum(residue * residue, axis=-1, keepdims=True) + epsilon)
        )
    return jnp.stack(found, axis=1)


def basis_of(chosen, counted, steering):
    count, slots = chosen.shape
    directions = steering.shape[0]
    onehot = (
        chosen[:, :, None] == lax.broadcasted_iota(jnp.int32, (count, slots, directions), 2)
    ).astype(f32)
    live = (lax.broadcasted_iota(jnp.int32, (count, slots), 1) < counted[:, None]).astype(f32)
    vectors = jnp.einsum("crn,na->cra", onehot, steering, precision=highest) * live[:, :, None]
    basis = orthonormal(vectors)
    return jnp.pad(basis, ((0, 0), (0, octet - slots), (0, 0)))


def per_device(samples, taps, steering, interferer_ids, ranks):
    antennas, width = samples.shape
    length = taps.shape[1]
    frames = width // length
    radix = length // lanes
    groups = radix // 2
    kept = lanes // 2
    shards = lax.axis_size("tm")
    spread = lax.axis_size("chan")
    devices = spread * shards
    owned = interferer_ids.shape[0]
    frame_total = frames * shards

    padded = samples
    if antennas < octet:
        padded = jnp.pad(samples, ((0, octet - antennas), (0, 0)))
    edge = lax.ppermute(
        padded[:, width - frame_block * length :],
        "tm",
        [(i, i + 1) for i in range(shards - 1)],
    )
    steps = frames // frame_block
    sections = filter_sections(padded, padded, taps, 1, steps - 1)
    sections = filter_sections(edge, padded, taps, 0, 1, sections)
    tables = [jnp.asarray(table) for table in phase_tables(length)]
    basis = basis_of(interferer_ids, ranks, steering)

    whole_runs = owned % radix == 0
    cuts = chunk_counts if whole_runs else (groups,)
    first = 0
    out = None
    for count in cuts:
        spectra = channels_of(sections, tables, first, count)
        bins = [
            k
            for g in range(first, first + count)
            for k in (g, radix - g if g else groups)
        ]
        runs = owned // radix
        if whole_runs:
            spectra = spectra.reshape(devices, runs * 2 * count, octet, lanes)

            def place(index, first=first, count=count):
                run = index // (2 * count)
                column = index - run * (2 * count)
                group = first + column // 2
                mirrored = jnp.where(group == 0, groups, radix - group)
                return run * radix + jnp.where(column % 2 == 0, group, mirrored)
        else:
            spectra = spectra[:, np.argsort(bins)].reshape(devices, owned, octet, lanes)

            def place(index):
                return index
        if antennas < octet:
            spectra = spectra[:, :, :antennas]
        received = lax.all_to_all(spectra, ("chan", "tm"), split_axis=0, concat_axis=0, tiled=True)
        channels = received.shape[1]
        received = received.reshape(spread, shards, channels, antennas, lanes)
        if antennas < octet:
            received = received.transpose(1, 2, 0, 3, 4).reshape(
                shards, channels, spread * antennas // octet, octet, lanes
            ).transpose(2, 0, 1, 3, 4)
        out = covariances(received, basis, place, frame_total, owned, out)
        first += count
    return out


chunk_counts = (2, 4, 5, 4, 1)


def solution(mesh):
    in_specs = (P("chan", "tm"), P(), P(), P(("chan", "tm"), None), P(("chan", "tm")))
    out_specs = P(("chan", "tm"), None, None, None)
    return jax.shard_map(
        per_device, mesh=mesh, in_specs=in_specs, out_specs=out_specs, check_vma=False
    )
```

```python
import functools
import math

import jax
import jax.numpy as jnp
import ml_dtypes
import numpy as np
from jax import lax
from jax.experimental import pallas as pl
from jax.experimental.pallas import tpu as pltpu
from jax.sharding import PartitionSpec as P

lanes = 128
octet = 8
frame_block = 16
epsilon = 1e-06
highest = lax.Precision.HIGHEST
f32 = jnp.float32
bf16 = jnp.bfloat16
vmem_bytes = 56 * 1024 * 1024


def real_transform(x):
    size = len(x)
    if size == 2:
        return [(x[0] + x[1], None), (x[0] - x[1], None)]
    even = real_transform(x[0::2])
    odd = real_transform(x[1::2])
    half = size // 2
    bins = [None] * (half + 1)
    bins[0] = (even[0][0] + odd[0][0], None)
    bins[half] = (even[0][0] - odd[0][0], None)
    bins[half // 2] = (even[half // 2][0], -odd[half // 2][0])
    for k in range(1, half // 2):
        er, ei = even[k]
        o_r, oi = odd[k]
        c = math.cos(2 * math.pi * k / size)
        s = math.sin(2 * math.pi * k / size)
        if 4 * k == half:
            tr = (o_r + oi) * c
            ti = (oi - o_r) * c
        else:
            tr = o_r * c + oi * s
            ti = oi * c - o_r * s
        bins[k] = (er + tr, ei + ti)
        bins[half - k] = (er - tr, ti - ei)
    return bins


def split_two(x):
    high = x.astype(bf16)
    low = (x - high.astype(f32)).astype(bf16)
    return high, low


def split_three(x):
    high = x.astype(bf16).astype(f32)
    rest = x - high
    middle = rest.astype(bf16).astype(f32)
    return high, middle, rest - middle


def filter_kernel(length, before_ref, block_ref, taps_ref, *rest):
    high_ref, low_ref, filtered, sections = rest[-4:]
    tap_count = taps_ref.shape[0]
    radix = length // lanes

    @pl.loop(0, radix)
    def _(part):
        spot = pl.multiple_of(part * lanes, lanes)
        taps = [
            jnp.broadcast_to(taps_ref[pl.ds(t, 1), pl.ds(spot, lanes)], (octet, lanes))
            for t in range(tap_count)
        ]

        def sample(frame):
            ref = block_ref if frame >= 0 else before_ref
            place = pl.multiple_of(spot + frame % frame_block * length, lanes)
            return ref[:, pl.ds(place, lanes)].astype(f32)

        window = [sample(frame) for frame in range(1 - tap_count, 0)]
        for frame in range(frame_block):
            window.append(sample(frame))
            total = taps[0] * window[0]
            for t in range(1, tap_count):
                total = total + taps[t] * window[t]
            filtered[part, frame * octet : (frame + 1) * octet, :] = total
            window.pop(0)

    @pl.loop(0, octet)
    def _(antenna):
        for half in range(frame_block // octet):
            rows = pl.ds(half * octet * octet + antenna, octet, stride=octet)
            bins = real_transform([filtered[part, rows, :] for part in range(radix)])
            kept = pl.ds(half * octet, octet)
            sections[0, kept, :] = bins[0][0]
            sections[1, kept, :] = bins[radix // 2][0]
            for k in range(1, radix // 2):
                sections[2 * k, kept, :] = bins[k][0]
                sections[2 * k + 1, kept, :] = bins[k][1]
        for group in range(radix // 2):
            for side in range(2):
                high, low = split_two(sections[2 * group + side])
                high_ref[group, antenna, :, side * lanes : (side + 1) * lanes] = high
                low_ref[group, antenna, :, side * lanes : (side + 1) * lanes] = low


def filter_sections(before, samples, taps, first, steps, previous=None):
    length = taps.shape[1]
    frames = samples.shape[1] // length
    groups = length // lanes // 2
    width = frame_block * length
    shape = jax.ShapeDtypeStruct((groups, octet, frames, 2 * lanes), bf16)
    block = pl.BlockSpec(
        (groups, octet, frame_block, 2 * lanes), lambda i: (0, 0, i + first, 0)
    )
    in_specs = [
        pl.BlockSpec((octet, width), lambda i: (0, i)),
        pl.BlockSpec((octet, width), lambda i: (0, i + first)),
        pl.BlockSpec(taps.shape, lambda i: (0, 0)),
    ]
    operands = [before, samples, taps]
    aliases = {}
    if previous is not None:
        in_specs += [pl.BlockSpec(memory_space=pl.ANY)] * 2
        operands += previous
        aliases = {3: 0, 4: 1}
    return pl.pallas_call(
        functools.partial(filter_kernel, length),
        grid=(steps,),
        in_specs=in_specs,
        out_specs=[block, block],
        out_shape=[shape, shape],
        scratch_shapes=[
            pltpu.VMEM((length // lanes, frame_block * octet, lanes), f32),
            pltpu.VMEM((length // lanes, frame_block, lanes), f32),
        ],
        input_output_aliases=aliases,
        compiler_params=pltpu.CompilerParams(vmem_limit_bytes=vmem_bytes),
        cost_estimate=pl.CostEstimate(
            flops=steps * 80_000_000, bytes_accessed=steps * 6_000_000, transcendentals=0
        ),
        name="filter_sections",
    )(*operands)


def phase_tables(length):
    radix = length // lanes
    kept = lanes // 2
    q = np.arange(lanes)
    m = np.arange(kept)

    def waves(k):
        angle = 2 * np.pi * (np.outer(q, k + radix * m) % length) / length
        return np.cos(angle), np.sin(angle)

    zero = np.zeros((lanes, kept))
    (c, s), (oc, os) = waves(0), waves(radix // 2)
    tables = [np.block([[c, zero, -s, zero], [zero, oc, zero, -os]])]
    for k in range(1, radix // 2):
        (c, s), (oc, os) = waves(k), waves(radix - k)
        tables.append(np.block([[c, oc, -s, -os], [s, -os, c, -oc]]))
    tables = np.stack(tables).astype(np.float32)
    high = tables.astype(ml_dtypes.bfloat16)
    low = (tables - high.astype(np.float32)).astype(ml_dtypes.bfloat16)
    return high, low


def contract_last(left, right):
    return lax.dot_general(left, right, (((1,), (1,)), ((), ())), preferred_element_type=f32)


def channel_kernel(high_ref, low_ref, wh_ref, wl_ref, out_ref, turned):
    frames = high_ref.shape[2]
    kept = wh_ref.shape[2] // 4
    rows = (octet * frames, 2 * lanes)
    high = high_ref[0].reshape(rows)
    low = low_ref[0].reshape(rows)
    dot = functools.partial(jnp.dot, preferred_element_type=f32)
    total = dot(high, wh_ref[0]) + (dot(low, wh_ref[0]) + dot(high, wl_ref[0]))
    for a in range(octet):
        piece = total[a * frames : (a + 1) * frames]
        piece = jnp.concatenate([piece[:, :lanes], piece[:, lanes:]], axis=0)
        turned[pl.ds(a, lanes, stride=octet), :] = piece.T
    for half in range(2):
        piece = turned[half * kept * octet : (half + 1) * kept * octet]
        out_ref[:, half] = piece.reshape(kept, octet, lanes).astype(bf16)


def channels_of(sections, tables, first, count):
    high, low = sections
    frames = high.shape[2]
    kept = lanes // 2
    section = pl.BlockSpec((1, octet, frames, 2 * lanes), lambda i: (i + first, 0, 0, 0))
    table = pl.BlockSpec((1, 2 * lanes, 2 * lanes), lambda i: (i + first, 0, 0))
    return pl.pallas_call(
        channel_kernel,
        grid=(count,),
        in_specs=[section, section, table, table],
        out_specs=pl.BlockSpec((kept, 2, octet, lanes), lambda i: (0, i, 0, 0)),
        out_shape=jax.ShapeDtypeStruct((kept, 2 * count, octet, lanes), bf16),
        scratch_shapes=[pltpu.VMEM((lanes * octet, lanes), f32)],
        compiler_params=pltpu.CompilerParams(vmem_limit_bytes=vmem_bytes),
        cost_estimate=pl.CostEstimate(
            flops=count * 400_000_000, bytes_accessed=count * 1_200_000, transcendentals=0
        ),
        name="channels_of",
    )(high, low, *tables)


def covariance_kernel(place, scale, x_ref, q_ref, *rest):
    out_ref, ready, done = rest[-3:]
    step = pl.program_id(0)
    steps = pl.num_programs(0)
    slot = lax.rem(step, 2)
    octets, shards, count = x_ref.shape[:3]
    antennas = octets * octet
    half = lanes // 2
    sign = jnp.where(lax.broadcasted_iota(jnp.int32, (1, lanes), 1) < half, 1.0, -1.0)

    def copies(at, which):
        return [
            pltpu.make_async_copy(
                ready.at[which, j], out_ref.at[place(at * count + j)], done.at[which, j]
            )
            for j in range(count)
        ]

    @pl.when(step >= 2)
    def _():
        for copy in copies(step - 2, slot):
            copy.wait()

    for j in range(count):
        pieces = [x_ref[:, t, j].astype(f32).reshape(antennas, lanes) for t in range(shards)]
        x = jnp.concatenate(pieces, axis=1)
        q = q_ref[place(step * count + j)]
        qh, qm, ql = split_three(q)
        left = jnp.concatenate([qh, qm, ql, jnp.zeros_like(q)], axis=0).astype(bf16)
        z = jnp.dot(left, x.astype(bf16), preferred_element_type=f32)
        z = z[:octet] + z[octet : 2 * octet] + z[2 * octet : 3 * octet]
        zh, zm, zl = split_three(z)
        left = jnp.concatenate([qh, qh, qm, qm, qh, ql], axis=0).astype(bf16)
        right = jnp.concatenate([zh, zm, zh, zm, zl, zh], axis=0).astype(bf16)
        y = x - lax.dot_general(left, right, (((0,), (0,)), ((), ())), preferred_element_type=f32)
        high, low = split_two(y)

        def turned(v):
            v = v.astype(f32)
            parts = [
                pltpu.roll(v[:, t * lanes : (t + 1) * lanes], half, 1) * sign for t in range(shards)
            ]
            return jnp.concatenate(parts, axis=1).astype(bf16)

        both = contract_last(
            jnp.concatenate([high, turned(high)], axis=0), jnp.concatenate([high, low], axis=0)
        )
        rest_ = contract_last(jnp.concatenate([low, turned(low)], axis=0), high)
        total = (both[:, :antennas] + (both[:, antennas:] + rest_)) * scale
        ready[slot, j] = total.reshape(2, antennas, antennas)

    for copy in copies(step, slot):
        copy.start()

    @pl.when(step == steps - 1)
    def _():
        @pl.when(step >= 1)
        def _():
            for copy in copies(step - 1, 1 - slot):
                copy.wait()

        for copy in copies(step, slot):
            copy.wait()


def covariances(received, basis, place, frame_total, total, previous):
    octets, shards, channels = received.shape[:3]
    antennas = octets * octet
    count = math.gcd(channels, 4)
    in_specs = [
        pl.BlockSpec((octets, shards, count, octet, lanes), lambda i: (0, 0, i, 0, 0)),
        pl.BlockSpec(basis.shape, lambda i: (0, 0, 0)),
    ]
    operands = [received, basis]
    aliases = {}
    if previous is not None:
        in_specs.append(pl.BlockSpec(memory_space=pl.ANY))
        operands.append(previous)
        aliases = {2: 0}
    return pl.pallas_call(
        functools.partial(covariance_kernel, place, 1.0 / frame_total),
        grid=(channels // count,),
        in_specs=in_specs,
        out_specs=pl.BlockSpec(memory_space=pl.ANY),
        out_shape=jax.ShapeDtypeStruct((total, 2, antennas, antennas), f32),
        scratch_shapes=[
            pltpu.VMEM((2, count, 2, antennas, antennas), f32),
            pltpu.SemaphoreType.DMA((2, count)),
        ],
        input_output_aliases=aliases,
        compiler_params=pltpu.CompilerParams(vmem_limit_bytes=vmem_bytes),
        cost_estimate=pl.CostEstimate(
            flops=channels * 60_000_000, bytes_accessed=channels * 250_000, transcendentals=0
        ),
        name="covariances",
    )(*operands)


def orthonormal(vectors):
    found = []
    for column in range(vectors.shape[1]):
        residue = vectors[:, column, :]
        for earlier in found:
            residue = residue - earlier * jnp.sum(earlier * residue, axis=-1, keepdims=True)
        found.append(
            residue / jnp.sqrt(jnp.sum(residue * residue, axis=-1, keepdims=True) + epsilon)
        )
    return jnp.stack(found, axis=1)


def basis_of(chosen, counted, steering):
    count, slots = chosen.shape
    directions = steering.shape[0]
    onehot = (
        chosen[:, :, None] == lax.broadcasted_iota(jnp.int32, (count, slots, directions), 2)
    ).astype(f32)
    live = (lax.broadcasted_iota(jnp.int32, (count, slots), 1) < counted[:, None]).astype(f32)
    vectors = jnp.einsum("crn,na->cra", onehot, steering, precision=highest) * live[:, :, None]
    basis = orthonormal(vectors)
    return jnp.pad(basis, ((0, 0), (0, octet - slots), (0, 0)))


def per_device(samples, taps, steering, interferer_ids, ranks):
    antennas, width = samples.shape
    length = taps.shape[1]
    frames = width // length
    radix = length // lanes
    groups = radix // 2
    kept = lanes // 2
    shards = lax.axis_size("tm")
    spread = lax.axis_size("chan")
    devices = spread * shards
    owned = interferer_ids.shape[0]
    frame_total = frames * shards

    padded = samples
    if antennas < octet:
        padded = jnp.pad(samples, ((0, octet - antennas), (0, 0)))
    edge = lax.ppermute(
        padded[:, width - frame_block * length :],
        "tm",
        [(i, i + 1) for i in range(shards - 1)],
    )
    steps = frames // frame_block
    sections = filter_sections(padded, padded, taps, 1, steps - 1)
    sections = filter_sections(edge, padded, taps, 0, 1, sections)
    tables = [jnp.asarray(table) for table in phase_tables(length)]
    basis = basis_of(interferer_ids, ranks, steering)

    whole_runs = owned % radix == 0
    cuts = chunk_counts if whole_runs else (groups,)
    first = 0
    out = None
    waiting = []

    def finish(out):
        received, place = waiting.pop(0)
        return covariances(received, basis, place, frame_total, owned, out)

    for count in cuts:
        spectra = channels_of(sections, tables, first, count)
        runs = owned // radix
        if whole_runs:
            spectra = spectra.reshape(devices, runs * 2 * count, octet, lanes)

            def place(index, first=first, count=count):
                run = index // (2 * count)
                column = index - run * (2 * count)
                group = first + column // 2
                mirrored = jnp.where(group == 0, groups, radix - group)
                return run * radix + jnp.where(column % 2 == 0, group, mirrored)
        else:
            bins = [k for g in range(groups) for k in (g, radix - g if g else groups)]
            spectra = spectra[:, np.argsort(bins)].reshape(devices, owned, octet, lanes)

            def place(index):
                return index
        if antennas < octet:
            spectra = spectra[:, :, :antennas]
        if len(waiting) == 2:
            out = finish(out)
            spectra, out = lax.optimization_barrier((spectra, out))
        received = lax.all_to_all(spectra, ("chan", "tm"), split_axis=0, concat_axis=0, tiled=True)
        channels = received.shape[1]
        received = received.reshape(spread, shards, channels, antennas, lanes)
        if antennas < octet:
            received = received.transpose(1, 2, 0, 3, 4).reshape(
                shards, channels, spread * antennas // octet, octet, lanes
            ).transpose(2, 0, 1, 3, 4)
        waiting.append((received, place))
        first += count
    while waiting:
        out = finish(out)
    return out


chunk_counts = (3, 5, 6, 2)


def solution(mesh):
    in_specs = (P("chan", "tm"), P(), P(), P(("chan", "tm"), None), P(("chan", "tm")))
    out_specs = P(("chan", "tm"), None, None, None)
    return jax.shard_map(
        per_device, mesh=mesh, in_specs=in_specs, out_specs=out_specs, check_vma=False
    )
```

```python
import functools
import math

import jax
import jax.numpy as jnp
import ml_dtypes
import numpy as np
from jax import lax
from jax.experimental import pallas as pl
from jax.experimental.pallas import tpu as pltpu
from jax.sharding import PartitionSpec as P

lanes = 128
octet = 8
frame_block = 16
epsilon = 1e-06
highest = lax.Precision.HIGHEST
f32 = jnp.float32
bf16 = jnp.bfloat16


def real_transform(x):
    size = len(x)
    if size == 2:
        return [(x[0] + x[1], None), (x[0] - x[1], None)]
    even = real_transform(x[0::2])
    odd = real_transform(x[1::2])
    half = size // 2
    bins = [None] * (half + 1)
    bins[0] = (even[0][0] + odd[0][0], None)
    bins[half] = (even[0][0] - odd[0][0], None)
    bins[half // 2] = (even[half // 2][0], -odd[half // 2][0])
    for k in range(1, half // 2):
        er, ei = even[k]
        o_r, oi = odd[k]
        c = math.cos(2 * math.pi * k / size)
        s = math.sin(2 * math.pi * k / size)
        if 4 * k == half:
            tr = (o_r + oi) * c
            ti = (oi - o_r) * c
        else:
            tr = o_r * c + oi * s
            ti = oi * c - o_r * s
        bins[k] = (er + tr, ei + ti)
        bins[half - k] = (er - tr, ti - ei)
    return bins


def split_two(x):
    high = x.astype(bf16)
    low = (x - high.astype(f32)).astype(bf16)
    return high, low


def split_three(x):
    high = x.astype(bf16).astype(f32)
    rest = x - high
    middle = rest.astype(bf16).astype(f32)
    return high, middle, rest - middle


def filter_frames(length, step, block_ref, taps_ref, high, low, filtered, sections, history):
    tap_count = taps_ref.shape[0]
    radix = length // lanes

    @pl.loop(0, radix)
    def _(part):
        spot = pl.multiple_of(part * lanes, lanes)
        taps = [
            jnp.broadcast_to(taps_ref[pl.ds(t, 1), pl.ds(spot, lanes)], (octet, lanes))
            for t in range(tap_count)
        ]
        window = [history[part, j] for j in range(tap_count - 1)]
        for frame in range(frame_block):
            place = pl.multiple_of(spot + frame * length, lanes)
            window.append(block_ref[:, pl.ds(place, lanes)].astype(f32))
            total = taps[0] * window[0]
            for t in range(1, tap_count):
                total = total + taps[t] * window[t]
            filtered[part, frame * octet : (frame + 1) * octet, :] = total
            window.pop(0)
        for j in range(tap_count - 1):
            history[part, j] = window[j]

    kept = pl.ds(pl.multiple_of(step * frame_block, frame_block), frame_block)

    @pl.loop(0, octet)
    def _(antenna):
        for half in range(frame_block // octet):
            rows = pl.ds(half * octet * octet + antenna, octet, stride=octet)
            bins = real_transform([filtered[part, rows, :] for part in range(radix)])
            here = pl.ds(half * octet, octet)
            sections[0, here, :] = bins[0][0]
            sections[1, here, :] = bins[radix // 2][0]
            for k in range(1, radix // 2):
                sections[2 * k, here, :] = bins[k][0]
                sections[2 * k + 1, here, :] = bins[k][1]
        for group in range(radix // 2):
            for side in range(2):
                first, second = split_two(sections[2 * group + side])
                high[group, antenna, kept, side * lanes : (side + 1) * lanes] = first
                low[group, antenna, kept, side * lanes : (side + 1) * lanes] = second


def second_stage(high, low, wh_ref, wl_ref):
    dot = functools.partial(jnp.dot, preferred_element_type=f32)
    return dot(high, wh_ref[0]) + (dot(low, wh_ref[0]) + dot(high, wl_ref[0]))


def head_kernel(length, steps, count, with_edge, *refs):
    before_ref, block_ref, taps_ref, wh_ref, wl_ref = refs[:5]
    refs = refs[5:]
    high_out, low_out = refs[:2]
    refs = refs[2:]
    if with_edge:
        edge_out, refs = refs[0], refs[1:]
    if count:
        out_ref, refs = refs[0], refs[1:]
    filtered, sections, history, turned, high, low, done = refs
    step = pl.program_id(0)
    frames = high.shape[2]
    radix = length // lanes
    kept = lanes // 2
    copies = [
        pltpu.make_async_copy(high.at[pl.ds(count, radix // 2 - count)], high_out, done.at[0]),
        pltpu.make_async_copy(low.at[pl.ds(count, radix // 2 - count)], low_out, done.at[1]),
    ]
    if with_edge:
        copies.append(pltpu.make_async_copy(block_ref, edge_out, done.at[2]))

    @pl.when(step == 0)
    def _():
        past = history.shape[1]

        @pl.loop(0, radix)
        def _(part):
            for j in range(past):
                place = pl.multiple_of(part * lanes + (frame_block - past + j) * length, lanes)
                history[part, j] = before_ref[:, pl.ds(place, lanes)].astype(f32)

    @pl.when(step < steps)
    def _():
        filter_frames(
            length, step, block_ref, taps_ref, high, low, filtered, sections, history
        )

    @pl.when(step == steps - 1)
    def _():
        for copy in copies:
            copy.start()

    if count:

        @pl.when(step >= steps)
        def _():
            group = step - steps
            rows = (octet * frames, 2 * lanes)
            total = second_stage(
                high[group].reshape(rows), low[group].reshape(rows), wh_ref, wl_ref
            )
            for a in range(octet):
                piece = total[a * frames : (a + 1) * frames]
                piece = jnp.concatenate([piece[:, :lanes], piece[:, lanes:]], axis=0).T
                piece = jnp.concatenate([piece[:kept], piece[kept:]], axis=1)
                turned[pl.ds(a, kept, stride=octet), :] = piece
            out_ref[:, 0] = turned[...].reshape(kept, octet, lanes).astype(bf16)

    @pl.when(step == steps + count - 1)
    def _():
        for copy in copies:
            copy.wait()


def head(before, before_block, samples, taps, tables, first, steps, count, with_edge):
    length = taps.shape[1]
    radix = length // lanes
    groups = radix // 2
    kept = lanes // 2
    frames = steps * frame_block
    width = frame_block * length
    rest = jax.ShapeDtypeStruct((groups - count, octet, frames, 2 * lanes), bf16)
    anywhere = pl.BlockSpec(memory_space=pl.ANY)
    table = pl.BlockSpec((1, 2 * lanes, 2 * lanes), lambda i: (jnp.maximum(i - steps, 0), 0, 0))
    out_shape, out_specs = [rest, rest], [anywhere, anywhere]
    if with_edge:
        out_shape.append(jax.ShapeDtypeStruct((octet, width), bf16))
        out_specs.append(anywhere)
    if count:
        out_shape.append(jax.ShapeDtypeStruct((kept, count, octet, lanes), bf16))
        out_specs.append(
            pl.BlockSpec((kept, 1, octet, lanes), lambda i: (0, jnp.maximum(i - steps, 0), 0, 0))
        )
    return pl.pallas_call(
        functools.partial(head_kernel, length, steps, count, with_edge),
        grid=(steps + count,),
        in_specs=[
            pl.BlockSpec((octet, width), lambda i: (0, before_block)),
            pl.BlockSpec((octet, width), lambda i: (0, first + jnp.minimum(i, steps - 1))),
            pl.BlockSpec(taps.shape, lambda i: (0, 0)),
            table,
            table,
        ],
        out_specs=out_specs,
        out_shape=out_shape,
        scratch_shapes=[
            pltpu.VMEM((radix, frame_block * octet, lanes), f32),
            pltpu.VMEM((radix, frame_block, lanes), f32),
            pltpu.VMEM((radix, taps.shape[0] - 1, octet, lanes), f32),
            pltpu.VMEM((kept * octet, lanes), f32),
            pltpu.VMEM((groups, octet, frames, 2 * lanes), bf16),
            pltpu.VMEM((groups, octet, frames, 2 * lanes), bf16),
            pltpu.SemaphoreType.DMA((3,)),
        ],
        compiler_params=pltpu.CompilerParams(vmem_limit_bytes=head_vmem),
        cost_estimate=pl.CostEstimate(
            flops=steps * 3_000_000_000 + count * 600_000_000,
            bytes_accessed=steps * 3_000_000,
            transcendentals=0,
        ),
        name="head",
    )(before, samples, taps, *tables)


def phase_tables(length):
    radix = length // lanes
    kept = lanes // 2
    q = np.arange(lanes)
    m = np.arange(kept)

    def waves(k):
        angle = 2 * np.pi * (np.outer(q, k + radix * m) % length) / length
        return np.cos(angle), np.sin(angle)

    zero = np.zeros((lanes, kept))
    (c, s), (oc, os) = waves(0), waves(radix // 2)
    tables = [np.block([[c, zero, -s, zero], [zero, oc, zero, -os]])]
    for k in range(1, radix // 2):
        (c, s), (oc, os) = waves(k), waves(radix - k)
        tables.append(np.block([[c, oc, -s, -os], [s, -os, c, -oc]]))
    tables = np.stack(tables).astype(np.float32)
    high = tables.astype(ml_dtypes.bfloat16)
    low = (tables - high.astype(np.float32)).astype(ml_dtypes.bfloat16)
    return high, low


def contract_last(left, right):
    return lax.dot_general(left, right, (((1,), (1,)), ((), ())), preferred_element_type=f32)


def channel_kernel(ha_ref, la_ref, hb_ref, lb_ref, wh_ref, wl_ref, out_ref, turned):
    frames = ha_ref.shape[2]
    kept = lanes // 2
    rows = (octet * frames, 2 * lanes)
    high = jnp.concatenate([ha_ref[0].reshape(rows), hb_ref[0].reshape(rows)], axis=0)
    low = jnp.concatenate([la_ref[0].reshape(rows), lb_ref[0].reshape(rows)], axis=0)
    total = second_stage(high, low, wh_ref, wl_ref)
    for a in range(octet):
        one = total[a * frames : (a + 1) * frames]
        two = total[(octet + a) * frames : (octet + a + 1) * frames]
        piece = [one[:, :lanes], two[:, :lanes], one[:, lanes:], two[:, lanes:]]
        turned[pl.ds(a, lanes, stride=octet), :] = jnp.concatenate(piece, axis=0).T
    for half in range(2):
        piece = turned[half * kept * octet : (half + 1) * kept * octet]
        out_ref[:, half] = piece.reshape(kept, octet, lanes).astype(bf16)


def channels_of(first_half, second_half, tables, skipped, first, count):
    frames = first_half[0].shape[2]
    kept = lanes // 2
    section = pl.BlockSpec((1, octet, frames, 2 * lanes), lambda i: (i + first - skipped, 0, 0, 0))
    table = pl.BlockSpec((1, 2 * lanes, 2 * lanes), lambda i: (i + first, 0, 0))
    return pl.pallas_call(
        channel_kernel,
        grid=(count,),
        in_specs=[section] * 4 + [table] * 2,
        out_specs=pl.BlockSpec((kept, 2, octet, lanes), lambda i: (0, i, 0, 0)),
        out_shape=jax.ShapeDtypeStruct((kept, 2 * count, octet, lanes), bf16),
        scratch_shapes=[pltpu.VMEM((lanes * octet, lanes), f32)],
        compiler_params=pltpu.CompilerParams(vmem_limit_bytes=channel_vmem),
        cost_estimate=pl.CostEstimate(
            flops=count * 800_000_000, bytes_accessed=count * 1_200_000, transcendentals=0
        ),
        name="channels_of",
    )(*first_half, *second_half, *tables)


def swap(one, two, width):
    lane = lax.broadcasted_iota(jnp.int32, (1, lanes), 1)
    even = lax.rem(lane // width, 2) == 0
    return (
        jnp.where(even, one, pltpu.roll(two, width, 1)),
        jnp.where(even, pltpu.roll(one, lanes - width, 1), two),
    )


def covariance_kernel(place, scale, halves, *refs):
    x_refs, q_ref = refs[:halves], refs[halves]
    out_ref, ready, done = refs[-3:]
    step = pl.program_id(0)
    steps = pl.num_programs(0)
    slot = lax.rem(step, 2)
    octets, shards, blocks = x_refs[0].shape[:3]
    antennas = octets * octet
    half = lanes // 2
    count = blocks * halves

    def copies(at, which):
        return [
            pltpu.make_async_copy(
                ready.at[which, j], out_ref.at[place(at * count + j)], done.at[which, j]
            )
            for j in range(count)
        ]

    @pl.when(step >= 2)
    def _():
        for copy in copies(step - 2, slot):
            copy.wait()

    def load(ref, t, j):
        if t >= shards:
            return jnp.zeros((antennas, lanes), f32)
        return ref[:, t, j].astype(f32).reshape(antennas, lanes)

    def channels(j):
        parts = [([], []) for _ in range(halves)]
        for t in range(0, shards, 2):
            if halves == 1:
                real, imag = swap(load(x_refs[0], t, j), load(x_refs[0], t + 1, j), half)
                parts[0][0].append(real)
                parts[0][1].append(imag)
            else:
                a0, a1 = (load(x_refs[0], u, j) for u in (t, t + 1))
                b0, b1 = (load(x_refs[1], u, j) for u in (t, t + 1))
                a0, b0 = swap(a0, b0, half)
                a1, b1 = swap(a1, b1, half)
                for found, pair in zip(parts, ((a0, a1), (b0, b1))):
                    real, imag = swap(*pair, half // 2)
                    found[0].append(real)
                    found[1].append(imag)
        return [jnp.concatenate(real + imag, axis=1) for real, imag in parts]

    def project(x, q):
        qh, qm, ql = split_three(q)
        left = jnp.concatenate([qh, qm, ql, jnp.zeros_like(q)], axis=0).astype(bf16)
        z = jnp.dot(left, x.astype(bf16), preferred_element_type=f32)
        z = z[:octet] + z[octet : 2 * octet] + z[2 * octet : 3 * octet]
        zh, zm, zl = split_three(z)
        left = jnp.concatenate([qh, qh, qm, qm, qh, ql], axis=0).astype(bf16)
        right = jnp.concatenate([zh, zm, zh, zm, zl, zh], axis=0).astype(bf16)
        return x - lax.dot_general(
            left, right, (((0,), (0,)), ((), ())), preferred_element_type=f32
        )

    def turned(v):
        middle = v.shape[1] // 2
        return jnp.concatenate([v[:, middle:], -v[:, :middle]], axis=1)

    for j in range(blocks):
        for h, x in enumerate(channels(j)):
            at = j * halves + h
            high, low = split_two(project(x, q_ref[place(step * count + at)]))
            left = jnp.concatenate([high, turned(high), low, turned(low)], axis=0)
            total = contract_last(left, jnp.concatenate([high, low], axis=0))
            total = total[:, :antennas] + total[:, antennas:]
            total = (total[: 2 * antennas] + total[2 * antennas :]) * scale
            ready[slot, at] = total.reshape(2, antennas, antennas)

    for copy in copies(step, slot):
        copy.start()

    @pl.when(step == steps - 1)
    def _():
        @pl.when(step >= 1)
        def _():
            for copy in copies(step - 1, 1 - slot):
                copy.wait()

        for copy in copies(step, slot):
            copy.wait()


def covariances(received, basis, place, frame_total, total, previous):
    halves = len(received)
    octets, shards, blocks = received[0].shape[:3]
    antennas = octets * octet
    count = math.gcd(blocks, 4 // halves)
    in_specs = [
        pl.BlockSpec((octets, shards, count, octet, lanes), lambda i: (0, 0, i, 0, 0))
    ] * halves
    in_specs.append(pl.BlockSpec(basis.shape, lambda i: (0, 0, 0)))
    operands = [*received, basis]
    aliases = {}
    if previous is not None:
        in_specs.append(pl.BlockSpec(memory_space=pl.ANY))
        operands.append(previous)
        aliases = {halves + 1: 0}
    return pl.pallas_call(
        functools.partial(covariance_kernel, place, 1.0 / frame_total, halves),
        grid=(blocks // count,),
        in_specs=in_specs,
        out_specs=pl.BlockSpec(memory_space=pl.ANY),
        out_shape=jax.ShapeDtypeStruct((total, 2, antennas, antennas), f32),
        scratch_shapes=[
            pltpu.VMEM((2, count * halves, 2, antennas, antennas), f32),
            pltpu.SemaphoreType.DMA((2, count * halves)),
        ],
        input_output_aliases=aliases,
        compiler_params=pltpu.CompilerParams(vmem_limit_bytes=covariance_vmem),
        cost_estimate=pl.CostEstimate(
            flops=blocks * halves * 400_000_000,
            bytes_accessed=blocks * halves * 250_000,
            transcendentals=0,
        ),
        name="covariances",
    )(*operands)


def orthonormal(vectors):
    found = []
    for column in range(vectors.shape[1]):
        residue = vectors[:, column, :]
        for earlier in found:
            residue = residue - earlier * jnp.sum(earlier * residue, axis=-1, keepdims=True)
        found.append(
            residue / jnp.sqrt(jnp.sum(residue * residue, axis=-1, keepdims=True) + epsilon)
        )
    return jnp.stack(found, axis=1)


def basis_of(chosen, counted, steering):
    count, slots = chosen.shape
    directions = steering.shape[0]
    onehot = (
        chosen[:, :, None] == lax.broadcasted_iota(jnp.int32, (count, slots, directions), 2)
    ).astype(f32)
    live = (lax.broadcasted_iota(jnp.int32, (count, slots), 1) < counted[:, None]).astype(f32)
    vectors = jnp.einsum("crn,na->cra", onehot, steering, precision=highest) * live[:, :, None]
    basis = orthonormal(vectors)
    return jnp.pad(basis, ((0, 0), (0, octet - slots), (0, 0)))


def per_device(samples, taps, steering, interferer_ids, ranks):
    antennas, width = samples.shape
    length = taps.shape[1]
    frames = width // length
    radix = length // lanes
    groups = radix // 2
    kept = lanes // 2
    shards = lax.axis_size("tm")
    spread = lax.axis_size("chan")
    devices = spread * shards
    owned = interferer_ids.shape[0]
    frame_total = frames * shards

    padded = samples
    if antennas < octet:
        padded = jnp.pad(samples, ((0, octet - antennas), (0, 0)))
    tables = [jnp.asarray(table) for table in phase_tables(length)]
    blocks = frames // frame_block
    middle = blocks // 2
    whole_runs = owned % radix == 0
    runs = owned // radix
    early, cuts = (early_pairs, later_pairs) if whole_runs else (0, (groups,))

    def exchange(spectra):
        received = lax.all_to_all(spectra, ("chan", "tm"), split_axis=0, concat_axis=0, tiled=True)
        received = received.reshape(spread, shards, -1, antennas, lanes)
        if antennas < octet:
            received = received.transpose(1, 2, 0, 3, 4).reshape(
                shards, -1, spread * antennas // octet, octet, lanes
            ).transpose(2, 0, 1, 3, 4)
        return received

    def channel_at(first, count):
        def place(index):
            run = index // (2 * count)
            column = index - run * (2 * count)
            group = first + column // 2
            mirrored = jnp.where(group == 0, groups, radix - group)
            return run * radix + jnp.where(column % 2 == 0, group, mirrored)

        return place

    late_high, late_low, edge, *spectra = head(
        padded, middle - 1, padded, taps, tables, middle, blocks - middle, early, True
    )
    before = lax.ppermute(edge, "tm", [(i, i + 1) for i in range(shards - 1)])
    waiting = []
    if early:
        late_early = exchange(spectra[0].reshape(devices, -1, octet, lanes))
    basis = basis_of(interferer_ids, ranks, steering)
    soon_high, soon_low, *spectra = head(
        before, 0, padded, taps, tables, 0, middle, early, False
    )
    first = early
    out = None
    for count in cuts:
        fresh = channels_of(
            (soon_high, soon_low), (late_high, late_low), tables, early, first, count
        )
        if whole_runs:
            fresh = fresh.reshape(devices, -1, octet, lanes)
            sent = fresh
            if first == early and early:
                head_rows = spectra[0].reshape(devices, -1, octet, lanes)
                sent = jnp.concatenate([head_rows, fresh], axis=1)
            if len(waiting) == 2 and not early:
                out = covariances(*waiting.pop(0), frame_total, owned, out)
                sent, out = lax.optimization_barrier((sent, out))
            elif early and first == early:
                sent, late_early = lax.optimization_barrier((sent, late_early))
            received = exchange(sent)
            if first == early and early:
                cut = runs * early
                waiting.append(
                    ((received[:, :, :cut], late_early), basis, channel_at(0, early))
                )
                received = received[:, :, cut:]
            waiting.append(((received,), basis, channel_at(first, count)))
        else:
            bins = [k for g in range(groups) for k in (g, radix - g if g else groups)]
            fresh = fresh[:, np.argsort(bins)].reshape(devices, owned, octet, lanes)
            received = exchange(fresh[:, :, :antennas])
            waiting.append(((received,), basis, lambda index: index))
        first += count
    while waiting:
        out = covariances(*waiting.pop(0), frame_total, owned, out)
    return out


early_pairs = 6
later_pairs = (7, 3)
head_vmem = 56 * 1024 * 1024
channel_vmem = 56 * 1024 * 1024
covariance_vmem = 56 * 1024 * 1024


def solution(mesh):
    in_specs = (P("chan", "tm"), P(), P(), P(("chan", "tm"), None), P(("chan", "tm")))
    out_specs = P(("chan", "tm"), None, None, None)
    return jax.shard_map(
        per_device, mesh=mesh, in_specs=in_specs, out_specs=out_specs, check_vma=False
    )
```

```python
import functools
import math

import jax
import jax.numpy as jnp
import ml_dtypes
import numpy as np
from jax import lax
from jax.experimental import pallas as pl
from jax.experimental.pallas import tpu as pltpu
from jax.sharding import PartitionSpec as P

lanes = 128
octet = 8
frame_block = 16
epsilon = 1e-06
highest = lax.Precision.HIGHEST
f32 = jnp.float32
bf16 = jnp.bfloat16


def real_transform(x):
    size = len(x)
    if size == 2:
        return [(x[0] + x[1], None), (x[0] - x[1], None)]
    even = real_transform(x[0::2])
    odd = real_transform(x[1::2])
    half = size // 2
    bins = [None] * (half + 1)
    bins[0] = (even[0][0] + odd[0][0], None)
    bins[half] = (even[0][0] - odd[0][0], None)
    bins[half // 2] = (even[half // 2][0], -odd[half // 2][0])
    for k in range(1, half // 2):
        er, ei = even[k]
        o_r, oi = odd[k]
        c = math.cos(2 * math.pi * k / size)
        s = math.sin(2 * math.pi * k / size)
        if 4 * k == half:
            tr = (o_r + oi) * c
            ti = (oi - o_r) * c
        else:
            tr = o_r * c + oi * s
            ti = oi * c - o_r * s
        bins[k] = (er + tr, ei + ti)
        bins[half - k] = (er - tr, ti - ei)
    return bins


def split_two(x):
    high = x.astype(bf16)
    low = (x - high.astype(f32)).astype(bf16)
    return high, low


def split_three(x):
    high = x.astype(bf16).astype(f32)
    rest = x - high
    middle = rest.astype(bf16).astype(f32)
    return high, middle, rest - middle


def filter_frames(length, step, block_ref, taps_ref, high, low, filtered, sections, history):
    tap_count = taps_ref.shape[0]
    radix = length // lanes

    @pl.loop(0, radix)
    def _(part):
        spot = pl.multiple_of(part * lanes, lanes)
        taps = [
            jnp.broadcast_to(taps_ref[pl.ds(t, 1), pl.ds(spot, lanes)], (octet, lanes))
            for t in range(tap_count)
        ]
        window = [history[part, j] for j in range(tap_count - 1)]
        for frame in range(frame_block):
            place = pl.multiple_of(spot + frame * length, lanes)
            window.append(block_ref[:, pl.ds(place, lanes)].astype(f32))
            total = taps[0] * window[0]
            for t in range(1, tap_count):
                total = total + taps[t] * window[t]
            filtered[part, frame * octet : (frame + 1) * octet, :] = total
            window.pop(0)
        for j in range(tap_count - 1):
            history[part, j] = window[j]

    kept = pl.ds(pl.multiple_of(step * frame_block, frame_block), frame_block)

    @pl.loop(0, octet)
    def _(antenna):
        for half in range(frame_block // octet):
            rows = pl.ds(half * octet * octet + antenna, octet, stride=octet)
            bins = real_transform([filtered[part, rows, :] for part in range(radix)])
            here = pl.ds(half * octet, octet)
            sections[0, here, :] = bins[0][0]
            sections[1, here, :] = bins[radix // 2][0]
            for k in range(1, radix // 2):
                sections[2 * k, here, :] = bins[k][0]
                sections[2 * k + 1, here, :] = bins[k][1]
        for group in range(radix // 2):
            for side in range(2):
                first, second = split_two(sections[2 * group + side])
                high[group, antenna, kept, side * lanes : (side + 1) * lanes] = first
                low[group, antenna, kept, side * lanes : (side + 1) * lanes] = second


def second_stage(high, low, wave_high, wave_low):
    dot = functools.partial(jnp.dot, preferred_element_type=f32)
    return dot(high, wave_high) + (dot(low, wave_high) + dot(high, wave_low))


def divisor(*sizes, most=3):
    return max(n for n in range(1, most + 1) if all(size % n == 0 for size in sizes))


def head_kernel(length, steps, count, with_edge, *refs):
    before_ref, block_ref, taps_ref, wh_ref, wl_ref = refs[:5]
    refs = refs[5:]
    high_out, low_out = refs[:2]
    refs = refs[2:]
    if with_edge:
        edge_out, refs = refs[0], refs[1:]
    if count:
        out_ref, refs = refs[0], refs[1:]
    filtered, sections, history, turned, high, low, done = refs
    step = pl.program_id(0)
    frames = high.shape[2]
    radix = length // lanes
    kept = lanes // 2
    copies = [
        pltpu.make_async_copy(high.at[pl.ds(count, radix // 2 - count)], high_out, done.at[0]),
        pltpu.make_async_copy(low.at[pl.ds(count, radix // 2 - count)], low_out, done.at[1]),
    ]
    if with_edge:
        copies.append(pltpu.make_async_copy(block_ref, edge_out, done.at[2]))

    @pl.when(step == 0)
    def _():
        past = history.shape[1]

        @pl.loop(0, radix)
        def _(part):
            for j in range(past):
                place = pl.multiple_of(part * lanes + (frame_block - past + j) * length, lanes)
                history[part, j] = before_ref[:, pl.ds(place, lanes)].astype(f32)

    @pl.when(step < steps)
    def _():
        filter_frames(
            length, step, block_ref, taps_ref, high, low, filtered, sections, history
        )

    @pl.when(step == steps - 1)
    def _():
        for copy in copies:
            copy.start()

    if count:

        @pl.when(step >= steps)
        def _():
            rows = (octet * frames, 2 * lanes)
            totals = []
            for j in range(turned.shape[0]):
                group = (step - steps) * turned.shape[0] + j
                pair = high[group].reshape(rows), low[group].reshape(rows)
                totals.append(second_stage(*pair, wh_ref[j], wl_ref[j]))
            for j, total in enumerate(totals):
                for a in range(octet):
                    piece = total[a * frames : (a + 1) * frames]
                    piece = jnp.concatenate([piece[:, :lanes], piece[:, lanes:]], axis=0).T
                    piece = jnp.concatenate([piece[:kept], piece[kept:]], axis=1)
                    turned[j, pl.ds(a, kept, stride=octet), :] = piece
            for j in range(turned.shape[0]):
                out_ref[:, j] = turned[j].reshape(kept, octet, lanes).astype(bf16)

    @pl.when(step == pl.num_programs(0) - 1)
    def _():
        for copy in copies:
            copy.wait()


def head(before, before_block, samples, taps, tables, first, steps, count, with_edge, columns):
    length = taps.shape[1]
    radix = length // lanes
    groups = radix // 2
    kept = lanes // 2
    frames = steps * frame_block
    width = frame_block * length
    rest = jax.ShapeDtypeStruct((groups - count, octet, frames, 2 * lanes), bf16)
    anywhere = pl.BlockSpec(memory_space=pl.ANY)
    each = divisor(count)
    table = pl.BlockSpec((each, 2 * lanes, 2 * lanes), lambda i: (jnp.maximum(i - steps, 0), 0, 0))
    out_shape, out_specs = [rest, rest], [anywhere, anywhere]
    if with_edge:
        out_shape.append(jax.ShapeDtypeStruct((octet, width), bf16))
        out_specs.append(anywhere)
    if count:
        out_shape.append(jax.ShapeDtypeStruct((kept, columns, octet, lanes), bf16))
        out_specs.append(
            pl.BlockSpec((kept, each, octet, lanes), lambda i: (0, jnp.maximum(i - steps, 0), 0, 0))
        )
    return pl.pallas_call(
        functools.partial(head_kernel, length, steps, count, with_edge),
        grid=(steps + count // each,),
        in_specs=[
            pl.BlockSpec((octet, width), lambda i: (0, before_block)),
            pl.BlockSpec((octet, width), lambda i: (0, first + jnp.minimum(i, steps - 1))),
            pl.BlockSpec(taps.shape, lambda i: (0, 0)),
            table,
            table,
        ],
        out_specs=out_specs,
        out_shape=out_shape,
        scratch_shapes=[
            pltpu.VMEM((radix, frame_block * octet, lanes), f32),
            pltpu.VMEM((radix, frame_block, lanes), f32),
            pltpu.VMEM((radix, taps.shape[0] - 1, octet, lanes), f32),
            pltpu.VMEM((each, kept * octet, lanes), f32),
            pltpu.VMEM((groups, octet, frames, 2 * lanes), bf16),
            pltpu.VMEM((groups, octet, frames, 2 * lanes), bf16),
            pltpu.SemaphoreType.DMA((3,)),
        ],
        compiler_params=pltpu.CompilerParams(vmem_limit_bytes=head_vmem),
        cost_estimate=pl.CostEstimate(
            flops=steps * 3_000_000_000 + count * 600_000_000,
            bytes_accessed=steps * 3_000_000,
            transcendentals=0,
        ),
        name="head",
    )(before, samples, taps, *tables)


def phase_tables(length):
    radix = length // lanes
    kept = lanes // 2
    q = np.arange(lanes)
    m = np.arange(kept)

    def waves(k):
        angle = 2 * np.pi * (np.outer(q, k + radix * m) % length) / length
        return np.cos(angle), np.sin(angle)

    zero = np.zeros((lanes, kept))
    (c, s), (oc, os) = waves(0), waves(radix // 2)
    tables = [np.block([[c, zero, -s, zero], [zero, oc, zero, -os]])]
    for k in range(1, radix // 2):
        (c, s), (oc, os) = waves(k), waves(radix - k)
        tables.append(np.block([[c, oc, -s, -os], [s, -os, c, -oc]]))
    tables = np.stack(tables).astype(np.float32)
    high = tables.astype(ml_dtypes.bfloat16)
    low = (tables - high.astype(np.float32)).astype(ml_dtypes.bfloat16)
    return high, low


def contract_last(left, right):
    return lax.dot_general(left, right, (((1,), (1,)), ((), ())), preferred_element_type=f32)


def channel_kernel(ha_ref, la_ref, hb_ref, lb_ref, wh_ref, wl_ref, *refs):
    out_ref, turned = refs[-2:]
    frames = ha_ref.shape[2]
    kept = lanes // 2
    rows = (octet * frames, 2 * lanes)
    totals = []
    for j in range(turned.shape[0]):
        high = jnp.concatenate([ha_ref[j].reshape(rows), hb_ref[j].reshape(rows)], axis=0)
        low = jnp.concatenate([la_ref[j].reshape(rows), lb_ref[j].reshape(rows)], axis=0)
        totals.append(second_stage(high, low, wh_ref[j], wl_ref[j]))
    for j, total in enumerate(totals):
        for a in range(octet):
            one = total[a * frames : (a + 1) * frames]
            two = total[(octet + a) * frames : (octet + a + 1) * frames]
            piece = [one[:, :lanes], two[:, :lanes], one[:, lanes:], two[:, lanes:]]
            turned[j, pl.ds(a, lanes, stride=octet), :] = jnp.concatenate(piece, axis=0).T
    for j in range(turned.shape[0]):
        for half in range(2):
            piece = turned[j, half * kept * octet : (half + 1) * kept * octet]
            out_ref[:, 2 * j + half] = piece.reshape(kept, octet, lanes).astype(bf16)


def channels_of(first_half, second_half, tables, skipped, first, count, begun=None):
    frames = first_half[0].shape[2]
    kept = lanes // 2
    held = 0 if begun is None else begun.shape[1] - 2 * count
    each = divisor(count, first, first - skipped, held // 2) if held % 2 == 0 else 0
    section = pl.BlockSpec(
        (each, octet, frames, 2 * lanes), lambda i: (i + (first - skipped) // each, 0, 0, 0)
    )
    table = pl.BlockSpec((each, 2 * lanes, 2 * lanes), lambda i: (i + first // each, 0, 0))
    operands = [*first_half, *second_half, *tables]
    in_specs = [section] * 4 + [table] * 2
    aliases = {}
    if begun is not None:
        aliases = {len(operands): 0}
        operands.append(begun)
        in_specs.append(pl.BlockSpec(memory_space=pl.ANY))
    return pl.pallas_call(
        channel_kernel,
        grid=(count // each,),
        in_specs=in_specs,
        out_specs=pl.BlockSpec(
            (kept, 2 * each, octet, lanes), lambda i: (0, i + held // (2 * each), 0, 0)
        ),
        out_shape=jax.ShapeDtypeStruct((kept, held + 2 * count, octet, lanes), bf16),
        scratch_shapes=[pltpu.VMEM((each, lanes * octet, lanes), f32)],
        input_output_aliases=aliases,
        compiler_params=pltpu.CompilerParams(vmem_limit_bytes=channel_vmem),
        cost_estimate=pl.CostEstimate(
            flops=count * 800_000_000, bytes_accessed=count * 1_200_000, transcendentals=0
        ),
        name="channels_of",
    )(*operands)


def swap(one, two, width):
    lane = lax.broadcasted_iota(jnp.int32, (1, lanes), 1)
    even = lax.rem(lane // width, 2) == 0
    return (
        jnp.where(even, one, pltpu.roll(two, width, 1)),
        jnp.where(even, pltpu.roll(one, lanes - width, 1), two),
    )


def covariance_kernel(place, scale, halves, *refs):
    x_refs, q_ref = refs[:halves], refs[halves]
    out_ref, ready, done = refs[-3:]
    step = pl.program_id(0)
    steps = pl.num_programs(0)
    slot = lax.rem(step, 2)
    octets, shards, blocks = x_refs[0].shape[:3]
    antennas = octets * octet
    half = lanes // 2
    count = blocks * halves

    def copies(at, which):
        return [
            pltpu.make_async_copy(
                ready.at[which, j], out_ref.at[place(at * count + j)], done.at[which, j]
            )
            for j in range(count)
        ]

    @pl.when(step >= 2)
    def _():
        for copy in copies(step - 2, slot):
            copy.wait()

    def load(ref, t, j):
        if t >= shards:
            return jnp.zeros((antennas, lanes), f32)
        return ref[:, t, j].astype(f32).reshape(antennas, lanes)

    def channels(j):
        parts = [([], []) for _ in range(halves)]
        for t in range(0, shards, 2):
            if halves == 1:
                real, imag = swap(load(x_refs[0], t, j), load(x_refs[0], t + 1, j), half)
                parts[0][0].append(real)
                parts[0][1].append(imag)
            else:
                a0, a1 = (load(x_refs[0], u, j) for u in (t, t + 1))
                b0, b1 = (load(x_refs[1], u, j) for u in (t, t + 1))
                a0, b0 = swap(a0, b0, half)
                a1, b1 = swap(a1, b1, half)
                for found, pair in zip(parts, ((a0, a1), (b0, b1))):
                    real, imag = swap(*pair, half // 2)
                    found[0].append(real)
                    found[1].append(imag)
        return [jnp.concatenate(real + imag, axis=1) for real, imag in parts]

    def turned(v):
        middle = v.shape[1] // 2
        return jnp.concatenate([v[:, middle:], -v[:, :middle]], axis=1)

    xs = [x for j in range(blocks) for x in channels(j)]
    qs = [split_three(q_ref[place(step * count + at)]) for at in range(count)]
    zs = []
    for x, (qh, qm, ql) in zip(xs, qs):
        left = jnp.concatenate([qh, qm, ql, jnp.zeros_like(qh)], axis=0).astype(bf16)
        z = jnp.dot(left, x.astype(bf16), preferred_element_type=f32)
        zs.append(split_three(z[:octet] + z[octet : 2 * octet] + z[2 * octet : 3 * octet]))
    parts = []
    for x, (qh, qm, ql), (zh, zm, zl) in zip(xs, qs, zs):
        left = jnp.concatenate([qh, qh, qm, qm, qh, ql], axis=0).astype(bf16)
        right = jnp.concatenate([zh, zm, zh, zm, zl, zh], axis=0).astype(bf16)
        taken = lax.dot_general(left, right, (((0,), (0,)), ((), ())), preferred_element_type=f32)
        parts.append(split_two(x - taken))
    for at, ((high, low), copy) in enumerate(zip(parts, copies(step, slot))):
        left = jnp.concatenate([high, turned(high), low, turned(low)], axis=0)
        total = contract_last(left, jnp.concatenate([high, low], axis=0))
        total = total[:, :antennas] + total[:, antennas:]
        total = (total[: 2 * antennas] + total[2 * antennas :]) * scale
        ready[slot, at] = total.reshape(2, antennas, antennas)
        copy.start()

    @pl.when(step == steps - 1)
    def _():
        @pl.when(step >= 1)
        def _():
            for copy in copies(step - 1, 1 - slot):
                copy.wait()

        for copy in copies(step, slot):
            copy.wait()


def covariances(received, basis, place, frame_total, total, previous):
    halves = len(received)
    array, runs, _, blocks = received[0]
    octets, shards = array.shape[:2]
    antennas = octets * octet
    sizes = [n for a, r, begin, _ in received for n in (a.shape[2] // r, begin)]
    count = divisor(blocks, *sizes, most=8 // halves)
    steps = blocks // count

    def window(array, runs, begin, _):
        stride = array.shape[2] // runs // count

        def index(i):
            run = i // steps
            return (0, 0, run * stride + begin // count + i - run * steps, 0, 0)

        return pl.BlockSpec((octets, shards, count, octet, lanes), index)

    in_specs = [window(*one) for one in received]
    in_specs.append(pl.BlockSpec(basis.shape, lambda i: (0, 0, 0)))
    operands = [*(one[0] for one in received), basis]
    aliases = {}
    if previous is not None:
        in_specs.append(pl.BlockSpec(memory_space=pl.ANY))
        operands.append(previous)
        aliases = {halves + 1: 0}
    return pl.pallas_call(
        functools.partial(covariance_kernel, place, 1.0 / frame_total, halves),
        grid=(runs * steps,),
        in_specs=in_specs,
        out_specs=pl.BlockSpec(memory_space=pl.ANY),
        out_shape=jax.ShapeDtypeStruct((total, 2, antennas, antennas), f32),
        scratch_shapes=[
            pltpu.VMEM((2, count * halves, 2, antennas, antennas), f32),
            pltpu.SemaphoreType.DMA((2, count * halves)),
        ],
        input_output_aliases=aliases,
        compiler_params=pltpu.CompilerParams(vmem_limit_bytes=covariance_vmem),
        cost_estimate=pl.CostEstimate(
            flops=runs * blocks * halves * 400_000_000,
            bytes_accessed=runs * blocks * halves * 250_000,
            transcendentals=0,
        ),
        name="covariances",
    )(*operands)


def orthonormal(vectors):
    found = []
    for column in range(vectors.shape[1]):
        residue = vectors[:, column, :]
        for earlier in found:
            residue = residue - earlier * jnp.sum(earlier * residue, axis=-1, keepdims=True)
        found.append(
            residue / jnp.sqrt(jnp.sum(residue * residue, axis=-1, keepdims=True) + epsilon)
        )
    return jnp.stack(found, axis=1)


def basis_of(chosen, counted, steering):
    count, slots = chosen.shape
    directions = steering.shape[0]
    onehot = (
        chosen[:, :, None] == lax.broadcasted_iota(jnp.int32, (count, slots, directions), 2)
    ).astype(f32)
    live = (lax.broadcasted_iota(jnp.int32, (count, slots), 1) < counted[:, None]).astype(f32)
    vectors = jnp.einsum("crn,na->cra", onehot, steering, precision=highest) * live[:, :, None]
    basis = orthonormal(vectors)
    return jnp.pad(basis, ((0, 0), (0, octet - slots), (0, 0)))


def per_device(samples, taps, steering, interferer_ids, ranks):
    antennas, width = samples.shape
    length = taps.shape[1]
    frames = width // length
    radix = length // lanes
    groups = radix // 2
    kept = lanes // 2
    shards = lax.axis_size("tm")
    spread = lax.axis_size("chan")
    devices = spread * shards
    owned = interferer_ids.shape[0]
    frame_total = frames * shards

    padded = samples
    if antennas < octet:
        padded = jnp.pad(samples, ((0, octet - antennas), (0, 0)))
    tables = [jnp.asarray(table) for table in phase_tables(length)]
    blocks = frames // frame_block
    middle = blocks // 2
    whole_runs = owned % radix == 0
    runs = owned // radix
    early, cuts = (early_pairs, later_pairs) if whole_runs else (0, (groups,))

    def exchange(spectra):
        received = lax.all_to_all(spectra, ("chan", "tm"), split_axis=0, concat_axis=0, tiled=True)
        received = received.reshape(spread, shards, -1, antennas, lanes)
        if antennas < octet:
            received = received.transpose(1, 2, 0, 3, 4).reshape(
                shards, -1, spread * antennas // octet, octet, lanes
            ).transpose(2, 0, 1, 3, 4)
        return received

    def channel_at(first, count):
        def place(index):
            run = index // (2 * count)
            column = index - run * (2 * count)
            group = first + column // 2
            mirrored = jnp.where(group == 0, groups, radix - group)
            return run * radix + jnp.where(column % 2 == 0, group, mirrored)

        return place

    late_high, late_low, edge, *spectra = head(
        padded, middle - 1, padded, taps, tables, middle, blocks - middle, early, True, early
    )
    before = lax.ppermute(edge, "tm", [(i, i + 1) for i in range(shards - 1)])
    if early:
        late_early = exchange(spectra[0].reshape(devices, -1, octet, lanes))
    basis = basis_of(interferer_ids, ranks, steering)
    soon_high, soon_low, *spectra = head(
        before, 0, padded, taps, tables, 0, middle, early, False, early + 2 * cuts[0]
    )
    first = early
    out = None
    waiting = []
    for count in cuts:
        begun = spectra[0] if early and first == early else None
        sent = channels_of(
            (soon_high, soon_low), (late_high, late_low), tables, early, first, count, begun
        )
        if whole_runs:
            sent = sent.reshape(devices, -1, octet, lanes)
            held = 0
            if begun is not None:
                sent, late_early = lax.optimization_barrier((sent, late_early))
                held = early
            else:
                sent, basis = lax.optimization_barrier((sent, basis))
            received = exchange(sent)
            if begun is not None:
                pieces = ((received, runs, 0, early), (late_early, runs, 0, early))
                waiting.append((pieces, basis, channel_at(0, early)))
            waiting.append(
                (((received, runs, held, 2 * count),), basis, channel_at(first, count))
            )
        else:
            bins = [k for g in range(groups) for k in (g, radix - g if g else groups)]
            sent = sent[:, np.argsort(bins)].reshape(devices, owned, octet, lanes)
            received = exchange(sent[:, :, :antennas])
            waiting.append((((received, 1, 0, owned),), basis, lambda index: index))
        first += count
    for one in waiting:
        out = covariances(*one, frame_total, owned, out)
    return out


early_pairs = 10
later_pairs = (3, 3)
head_vmem = 56 * 1024 * 1024
channel_vmem = 56 * 1024 * 1024
covariance_vmem = 24 * 1024 * 1024


def solution(mesh):
    in_specs = (P("chan", "tm"), P(), P(), P(("chan", "tm"), None), P(("chan", "tm")))
    out_specs = P(("chan", "tm"), None, None, None)
    return jax.shard_map(
        per_device, mesh=mesh, in_specs=in_specs, out_specs=out_specs, check_vma=False
    )
```

```python
import functools
import math

import jax
import jax.numpy as jnp
import ml_dtypes
import numpy as np
from jax import lax
from jax.experimental import pallas as pl
from jax.experimental.pallas import tpu as pltpu
from jax.sharding import PartitionSpec as P

lanes = 128
octet = 8
frame_block = 16
epsilon = 1e-06
highest = lax.Precision.HIGHEST
f32 = jnp.float32
bf16 = jnp.bfloat16


def real_transform(x):
    size = len(x)
    if size == 2:
        return [(x[0] + x[1], None), (x[0] - x[1], None)]
    even = real_transform(x[0::2])
    odd = real_transform(x[1::2])
    half = size // 2
    bins = [None] * (half + 1)
    bins[0] = (even[0][0] + odd[0][0], None)
    bins[half] = (even[0][0] - odd[0][0], None)
    bins[half // 2] = (even[half // 2][0], -odd[half // 2][0])
    for k in range(1, half // 2):
        er, ei = even[k]
        o_r, oi = odd[k]
        c = math.cos(2 * math.pi * k / size)
        s = math.sin(2 * math.pi * k / size)
        if 4 * k == half:
            tr = (o_r + oi) * c
            ti = (oi - o_r) * c
        else:
            tr = o_r * c + oi * s
            ti = oi * c - o_r * s
        bins[k] = (er + tr, ei + ti)
        bins[half - k] = (er - tr, ti - ei)
    return bins


def split_two(x):
    high = x.astype(bf16)
    low = (x - high.astype(f32)).astype(bf16)
    return high, low


def split_three(x):
    high = x.astype(bf16).astype(f32)
    rest = x - high
    middle = rest.astype(bf16).astype(f32)
    return high, middle, rest - middle


def filter_frames(length, step, block_ref, taps_ref, high, low, filtered, sections, history):
    tap_count = taps_ref.shape[0]
    radix = length // lanes

    @pl.loop(0, radix)
    def _(part):
        spot = pl.multiple_of(part * lanes, lanes)
        taps = [
            jnp.broadcast_to(taps_ref[pl.ds(t, 1), pl.ds(spot, lanes)], (octet, lanes))
            for t in range(tap_count)
        ]
        past = tap_count - 1
        window = [history[part, j] for j in range(past)]
        for frame in range(frame_block):
            place = pl.multiple_of(spot + frame * length, lanes)
            window.append(block_ref[:, pl.ds(place, lanes)].astype(f32))
        for j in range(past):
            history[part, j] = window[frame_block + j]

        def convolve(weights, values):
            sums = []
            for j in range(len(values) - len(weights) + 1):
                total = weights[-1] * values[j]
                for i in range(1, len(weights)):
                    total = total + weights[-1 - i] * values[j + i]
                sums.append(total)
            return sums

        even_taps, odd_taps = taps[past::-2], taps[past - 1 :: -2]
        odd = window[0::2]
        even = window[1::2]
        evens = convolve(even_taps, even)
        odds = convolve(odd_taps, odd)
        both_taps = [one + two for one, two in zip(even_taps, odd_taps)]
        both = convolve(both_taps, [one + two for one, two in zip(even, odd[1:])])
        for j in range(frame_block // 2):
            pair = (evens[j] + odds[j], both[j] - evens[j] - odds[j + 1])
            for frame, total in zip((2 * j, 2 * j + 1), pair):
                filtered[part, frame * octet : (frame + 1) * octet, :] = total

    kept = pl.ds(pl.multiple_of(step * frame_block, frame_block), frame_block)

    @pl.loop(0, octet)
    def _(antenna):
        for half in range(frame_block // octet):
            rows = pl.ds(half * octet * octet + antenna, octet, stride=octet)
            bins = real_transform([filtered[part, rows, :] for part in range(radix)])
            here = pl.ds(half * octet, octet)
            sections[0, here, :] = bins[0][0]
            sections[1, here, :] = bins[radix // 2][0]
            for k in range(1, radix // 2):
                sections[2 * k, here, :] = bins[k][0]
                sections[2 * k + 1, here, :] = bins[k][1]
        for group in range(radix // 2):
            for side in range(2):
                first, second = split_two(sections[2 * group + side])
                high[group, antenna, kept, side * lanes : (side + 1) * lanes] = first
                low[group, antenna, kept, side * lanes : (side + 1) * lanes] = second


def second_stage(high, low, wave_high, wave_low):
    dot = functools.partial(jnp.dot, preferred_element_type=f32)
    return dot(high, wave_high) + (dot(low, wave_high) + dot(high, wave_low))


def divisor(*sizes, most=3):
    return max(n for n in range(1, most + 1) if all(size % n == 0 for size in sizes))


def swap(one, two, width):
    lane = lax.broadcasted_iota(jnp.int32, (1, lanes), 1)
    even = lax.rem(lane // width, 2) == 0
    return (
        jnp.where(even, one, pltpu.roll(two, width, 1)),
        jnp.where(even, pltpu.roll(one, lanes - width, 1), two),
    )


def head_kernel(length, steps, each, size, skipped, with_edge, *refs):
    before_ref, block_ref, taps_ref, wave_high_ref, wave_low_ref = refs[:5]
    refs = refs[5:]
    if with_edge:
        edge_out, refs = refs[0], refs[1:]
    out_ref, refs = refs[0], refs[1:]
    filtered, sections, history, turned, high, low, wave_high, wave_low, done = refs
    step = pl.program_id(0)
    frames = high.shape[2]
    radix = length // lanes
    kept = lanes // 2
    taken = pl.ds(2 * skipped, 2 * size)
    waves = [
        pltpu.make_async_copy(wave_high_ref.at[taken], wave_high, done.at[1]),
        pltpu.make_async_copy(wave_low_ref.at[taken], wave_low, done.at[2]),
    ]
    edge = pltpu.make_async_copy(block_ref, edge_out, done.at[0]) if with_edge else None

    @pl.when(step == 0)
    def _():
        for copy in waves:
            copy.start()
        past = history.shape[1]

        @pl.loop(0, radix)
        def _(part):
            for j in range(past):
                place = pl.multiple_of(part * lanes + (frame_block - past + j) * length, lanes)
                history[part, j] = before_ref[:, pl.ds(place, lanes)].astype(f32)

    @pl.when(step < steps)
    def _():
        filter_frames(
            length, step, block_ref, taps_ref, high, low, filtered, sections, history
        )

    if with_edge:

        @pl.when(step == steps - 1)
        def _():
            edge.start()

    @pl.when(step == steps)
    def _():
        for copy in waves:
            copy.wait()

    @pl.when(step >= steps)
    def _():
        rows = (octet * frames, 2 * lanes)
        totals = []
        for j in range(2 * each):
            at = (step - steps) * 2 * each + j
            pair = high[2 * skipped + at].reshape(rows), low[2 * skipped + at].reshape(rows)
            totals.append(second_stage(*pair, wave_high[at], wave_low[at]))
        for j in range(each):
            for block in range(steps):
                for a in range(0, octet, 2):
                    piece = []
                    for at in (a, a + 1):
                        begin = at * frames + block * frame_block
                        for total in totals[2 * j : 2 * j + 2]:
                            part = total[begin : begin + frame_block]
                            piece += [part[:, :lanes], part[:, lanes:]]
                    piece = jnp.concatenate(piece, axis=0).T
                    one, two = swap(piece[:kept], piece[kept:], kept)
                    turned[j * steps + block, pl.ds(a, kept, stride=octet), :] = one
                    turned[j * steps + block, pl.ds(a + 1, kept, stride=octet), :] = two
        for j in range(each * steps):
            out_ref[:, j] = turned[j].reshape(kept, octet, lanes).astype(bf16)

    if with_edge:

        @pl.when(step == pl.num_programs(0) - 1)
        def _():
            edge.wait()


def head(before, before_block, samples, taps, tables, first, steps, skipped, size, with_edge):
    length = taps.shape[1]
    radix = length // lanes
    groups = radix // 2
    kept = lanes // 2
    frames = steps * frame_block
    width = frame_block * length
    each = divisor(size, skipped, most=2 if steps == 1 else 1)
    anywhere = pl.BlockSpec(memory_space=pl.ANY)
    out_shape, out_specs = [], []
    if with_edge:
        out_shape.append(jax.ShapeDtypeStruct((octet, width), bf16))
        out_specs.append(anywhere)
    out_shape.append(jax.ShapeDtypeStruct((kept, size * steps, octet, lanes), bf16))
    out_specs.append(
        pl.BlockSpec(
            (kept, each * steps, octet, lanes), lambda i: (0, jnp.maximum(i - steps, 0), 0, 0)
        )
    )
    return pl.pallas_call(
        functools.partial(head_kernel, length, steps, each, size, skipped, with_edge),
        grid=(steps + size // each,),
        in_specs=[
            pl.BlockSpec((octet, width), lambda i: (0, before_block)),
            pl.BlockSpec((octet, width), lambda i: (0, first + jnp.minimum(i, steps - 1))),
            pl.BlockSpec(taps.shape, lambda i: (0, 0)),
            anywhere,
            anywhere,
        ],
        out_specs=out_specs,
        out_shape=out_shape,
        scratch_shapes=[
            pltpu.VMEM((radix, frame_block * octet, lanes), f32),
            pltpu.VMEM((radix, frame_block, lanes), f32),
            pltpu.VMEM((radix, taps.shape[0] - 1, octet, lanes), f32),
            pltpu.VMEM((each * steps, kept * octet, lanes), f32),
            pltpu.VMEM((groups, octet, frames, 2 * lanes), bf16),
            pltpu.VMEM((groups, octet, frames, 2 * lanes), bf16),
            pltpu.VMEM((2 * size, 2 * lanes, 2 * lanes), bf16),
            pltpu.VMEM((2 * size, 2 * lanes, 2 * lanes), bf16),
            pltpu.SemaphoreType.DMA((3,)),
        ],
        compiler_params=pltpu.CompilerParams(vmem_limit_bytes=later_vmem if skipped else head_vmem),
        cost_estimate=pl.CostEstimate(
            flops=steps * 1_000_000_000, bytes_accessed=steps * 1_000_000, transcendentals=0
        ),
        name="head",
    )(before, samples, taps, *tables)


def phase_tables(length):
    radix = length // lanes
    kept = lanes // 2
    q = np.arange(lanes)
    m = np.arange(kept)

    def waves(k):
        angle = 2 * np.pi * (np.outer(q, k + radix * m) % length) / length
        return np.cos(angle), np.sin(angle)

    zero = np.zeros((lanes, kept))
    (c, s), (oc, os) = waves(0), waves(radix // 2)
    tables = [np.block([[c, zero, -s, zero], [zero, oc, zero, -os]])]
    for k in range(1, radix // 2):
        (c, s), (oc, os) = waves(k), waves(radix - k)
        tables.append(np.block([[c, oc, -s, -os], [s, -os, c, -oc]]))
    tables = np.stack(tables).astype(np.float32)
    high = tables.astype(ml_dtypes.bfloat16)
    low = (tables - high.astype(np.float32)).astype(ml_dtypes.bfloat16)
    return high, low


def contract_last(left, right):
    return lax.dot_general(left, right, (((1,), (1,)), ((), ())), preferred_element_type=f32)


def covariance_kernel(place, scale, widths, *refs):
    x_refs, q_ref = refs[: len(widths)], refs[len(widths)]
    packed = len(widths) > 1
    out_ref, ready, done = refs[-3:]
    step = pl.program_id(0)
    steps = pl.num_programs(0)
    slot = lax.rem(step, 2)
    octets, shards = x_refs[0].shape[:2]
    antennas = octets * octet
    columns = x_refs[0].shape[2] // widths[0]
    count = columns * (4 if packed else 1)

    def copies(at, which):
        return [
            pltpu.make_async_copy(
                ready.at[which, j], out_ref.at[place(at * count + j)], done.at[which, j]
            )
            for j in range(count)
        ]

    @pl.when(step >= 2)
    def _():
        for copy in copies(step - 2, slot):
            copy.wait()

    def load(ref, t, j):
        if t >= shards:
            return jnp.zeros((antennas, lanes), f32)
        return ref[:, t, j].astype(f32).reshape(antennas, lanes)

    def channels(j):
        parts = [[] for _ in range(8 if packed else 2)]
        for t in range(0, shards, 2):
            tiles = [
                load(ref, u, j * width + at)
                for u in (t, t + 1)
                for ref, width in zip(x_refs, widths)
                for at in range(width)
            ]
            stride = len(tiles) // 2
            while stride:
                for low in range(len(tiles)):
                    if not low & stride:
                        tiles[low], tiles[low + stride] = swap(
                            tiles[low], tiles[low + stride], lanes * stride // len(tiles)
                        )
                stride //= 2
            for part, tile in zip(parts, tiles):
                part.append(tile)
        return [
            jnp.concatenate(real + imag, axis=1) for real, imag in zip(parts[0::2], parts[1::2])
        ]

    def turned(v):
        middle = v.shape[1] // 2
        return jnp.concatenate([v[:, middle:], -v[:, :middle]], axis=1)

    xs = [x for j in range(columns) for x in channels(j)]
    qs = [split_three(q_ref[place(step * count + at)]) for at in range(count)]
    zs = []
    for x, (qh, qm, ql) in zip(xs, qs):
        left = jnp.concatenate([qh, qm, ql, jnp.zeros_like(qh)], axis=0).astype(bf16)
        z = jnp.dot(left, x.astype(bf16), preferred_element_type=f32)
        zs.append(split_three(z[:octet] + z[octet : 2 * octet] + z[2 * octet : 3 * octet]))
    parts = []
    for x, (qh, qm, ql), (zh, zm, zl) in zip(xs, qs, zs):
        left = jnp.concatenate([qh, qh, qm, qm, qh, ql], axis=0).astype(bf16)
        right = jnp.concatenate([zh, zm, zh, zm, zl, zh], axis=0).astype(bf16)
        taken = lax.dot_general(left, right, (((0,), (0,)), ((), ())), preferred_element_type=f32)
        parts.append(split_two(x - taken))
    for at, ((high, low), copy) in enumerate(zip(parts, copies(step, slot))):
        left = jnp.concatenate([high, turned(high), low, turned(low)], axis=0)
        total = contract_last(left, jnp.concatenate([high, low], axis=0))
        total = total[:, :antennas] + total[:, antennas:]
        total = (total[: 2 * antennas] + total[2 * antennas :]) * scale
        ready[slot, at] = total.reshape(2, antennas, antennas)
        copy.start()

    @pl.when(step == steps - 1)
    def _():
        @pl.when(step >= 1)
        def _():
            for copy in copies(step - 1, 1 - slot):
                copy.wait()

        for copy in copies(step, slot):
            copy.wait()


def covariances(received, basis, place, frame_total, total, previous, last):
    array, runs, _, taken, _ = received[0]
    octets, shards = array.shape[:2]
    antennas = octets * octet
    widths = [one[4] for one in received]
    sizes = [n for a, r, begin, _, width in received for n in (a.shape[2] // (r * width), begin)]
    packed = len(received) > 1
    each = divisor(taken, *sizes, most=2 if packed else 8)
    count = each * (4 if packed else 1)
    steps = taken // each

    def window(array, runs, begin, _, width):
        stride = array.shape[2] // (runs * width * each)

        def index(i):
            run = i // steps
            return (0, 0, run * stride + begin // each + i - run * steps, 0, 0)

        return pl.BlockSpec((octets, shards, each * width, octet, lanes), index)

    in_specs = [window(*one) for one in received]
    in_specs.append(pl.BlockSpec(basis.shape, lambda i: (0, 0, 0)))
    operands = [*(one[0] for one in received), basis]
    aliases = {}
    if previous is not None:
        in_specs.append(pl.BlockSpec(memory_space=pl.ANY))
        aliases = {len(operands): 0}
        operands.append(previous)
    return pl.pallas_call(
        functools.partial(covariance_kernel, place, 1.0 / frame_total, widths),
        grid=(runs * steps,),
        in_specs=in_specs,
        out_specs=pl.BlockSpec(memory_space=pl.ANY),
        out_shape=jax.ShapeDtypeStruct((total, 2, antennas, antennas), f32),
        scratch_shapes=[
            pltpu.VMEM((2, count, 2, antennas, antennas), f32),
            pltpu.SemaphoreType.DMA((2, count)),
        ],
        input_output_aliases=aliases,
        compiler_params=pltpu.CompilerParams(vmem_limit_bytes=last_vmem if last else covariance_vmem),
        cost_estimate=pl.CostEstimate(
            flops=runs * steps * count * 200_000_000,
            bytes_accessed=runs * steps * count * 200_000,
            transcendentals=0,
        ),
        name="covariances",
    )(*operands)


def orthonormal(vectors):
    found = []
    for column in range(vectors.shape[1]):
        residue = vectors[:, column, :]
        for earlier in found:
            residue = residue - earlier * jnp.sum(earlier * residue, axis=-1, keepdims=True)
        found.append(
            residue / jnp.sqrt(jnp.sum(residue * residue, axis=-1, keepdims=True) + epsilon)
        )
    return jnp.stack(found, axis=1)


def basis_of(chosen, counted, steering):
    count, slots = chosen.shape
    directions = steering.shape[0]
    onehot = (
        chosen[:, :, None] == lax.broadcasted_iota(jnp.int32, (count, slots, directions), 2)
    ).astype(f32)
    live = (lax.broadcasted_iota(jnp.int32, (count, slots), 1) < counted[:, None]).astype(f32)
    vectors = jnp.einsum("crn,na->cra", onehot, steering, precision=highest) * live[:, :, None]
    basis = orthonormal(vectors)
    return jnp.pad(basis, ((0, 0), (0, octet - slots), (0, 0)))


def per_device(samples, taps, steering, interferer_ids, ranks):
    antennas, width = samples.shape
    length = taps.shape[1]
    frames = width // length
    radix = length // lanes
    groups = radix // 2
    kept = lanes // 2
    shards = lax.axis_size("tm")
    spread = lax.axis_size("chan")
    devices = spread * shards
    owned = interferer_ids.shape[0]
    frame_total = frames * shards

    padded = samples
    if antennas < octet:
        padded = jnp.pad(samples, ((0, octet - antennas), (0, 0)))
    tables = [jnp.asarray(table) for table in phase_tables(length)]
    blocks = frames // frame_block
    whole_runs = owned % radix == 0
    runs = owned // radix
    twos = groups // 2
    cuts = (twos - last_twos, last_twos) if whole_runs else (twos,)

    def exchange(spectra):
        received = lax.all_to_all(spectra, ("chan", "tm"), split_axis=0, concat_axis=0, tiled=True)
        received = received.reshape(spread, shards, -1, antennas, lanes)
        if antennas < octet:
            received = received.transpose(1, 2, 0, 3, 4).reshape(
                shards, -1, spread * antennas // octet, octet, lanes
            ).transpose(2, 0, 1, 3, 4)
        return received

    def channel_at(first, count):
        def place(index):
            run = index // (4 * count)
            two = (index - run * (4 * count)) // 4
            group = 2 * (first + two) + index % 2
            mirrored = jnp.where(group == 0, groups, radix - group)
            return run * radix + jnp.where(index % 4 < 2, group, mirrored)

        return place

    edge, early = head(padded, blocks - 2, padded, taps, tables, blocks - 1, 1, 0, twos, True)
    before = lax.ppermute(edge, "tm", [(i, i + 1) for i in range(shards - 1)])
    if whole_runs:
        arrived = exchange(early.reshape(devices, -1, octet, lanes))
    basis = basis_of(interferer_ids, ranks, steering)

    def later(first, count):
        return head(before, 0, padded, taps, tables, 0, blocks - 1, first, count, False)[0]

    out = None
    if whole_runs:
        first = 0
        pieces = []
        for count in cuts:
            if first:
                before, basis = lax.optimization_barrier((before, basis))
            sent = later(first, count).reshape(devices, -1, octet, lanes)
            if not first:
                sent, arrived = lax.optimization_barrier((sent, arrived))
            pieces.append((exchange(sent), first, count))
            first += count
        for received, first, count in pieces:
            parts = (
                (received, runs, 0, count, blocks - 1),
                (arrived, runs, first, count, 1),
            )
            out = covariances(
                parts, basis, channel_at(first, count), frame_total, owned, out, first > 0
            )
    else:
        tiles = jnp.concatenate(
            [
                later(0, twos).reshape(kept, twos, blocks - 1, octet, 4, 2, frame_block),
                early.reshape(kept, twos, 1, octet, 4, 2, frame_block),
            ],
            axis=2,
        )
        tiles = tiles.transpose(0, 1, 4, 3, 5, 2, 6).reshape(kept, radix, octet, lanes)
        order = [
            k
            for g in range(0, groups, 2)
            for k in (g, g + 1, radix - g if g else groups, radix - g - 1)
        ]
        tiles = tiles[:, np.argsort(order), :antennas].reshape(devices, owned, antennas, lanes)
        received = exchange(tiles)
        parts = ((received, 1, 0, owned, 1),)
        out = covariances(parts, basis, lambda index: index, frame_total, owned, None, True)
    return out


last_twos = 2
head_vmem = 56 * 1024 * 1024
later_vmem = 32 * 1024 * 1024
covariance_vmem = 24 * 1024 * 1024
last_vmem = 24 * 1024 * 1024


def solution(mesh):
    in_specs = (P("chan", "tm"), P(), P(), P(("chan", "tm"), None), P(("chan", "tm")))
    out_specs = P(("chan", "tm"), None, None, None)
    return jax.shard_map(
        per_device, mesh=mesh, in_specs=in_specs, out_specs=out_specs, check_vma=False
    )
```

```python
import functools
import math

import jax
import jax.numpy as jnp
import ml_dtypes
import numpy as np
from jax import lax
from jax.experimental import pallas as pl
from jax.experimental.pallas import tpu as pltpu
from jax.sharding import PartitionSpec as P

lanes = 128
octet = 8
frame_block = 16
epsilon = 1e-06
highest = lax.Precision.HIGHEST
f32 = jnp.float32
bf16 = jnp.bfloat16


def real_transform(x):
    size = len(x)
    if size == 2:
        return [(x[0] + x[1], None), (x[0] - x[1], None)]
    even = real_transform(x[0::2])
    odd = real_transform(x[1::2])
    half = size // 2
    bins = [None] * (half + 1)
    bins[0] = (even[0][0] + odd[0][0], None)
    bins[half] = (even[0][0] - odd[0][0], None)
    bins[half // 2] = (even[half // 2][0], -odd[half // 2][0])
    for k in range(1, half // 2):
        er, ei = even[k]
        o_r, oi = odd[k]
        c = math.cos(2 * math.pi * k / size)
        s = math.sin(2 * math.pi * k / size)
        if 4 * k == half:
            tr = (o_r + oi) * c
            ti = (oi - o_r) * c
        else:
            tr = o_r * c + oi * s
            ti = oi * c - o_r * s
        bins[k] = (er + tr, ei + ti)
        bins[half - k] = (er - tr, ti - ei)
    return bins


def split_two(x):
    high = x.astype(bf16)
    low = (x - high.astype(f32)).astype(bf16)
    return high, low


def split_three(x):
    high = x.astype(bf16).astype(f32)
    rest = x - high
    middle = rest.astype(bf16).astype(f32)
    return high, middle, rest - middle


def filter_frames(length, step, before_ref, block_ref, taps_ref, high, low, filtered, sections, history):
    tap_count = taps_ref.shape[0]
    radix = length // lanes

    @pl.loop(0, radix, unroll=2)
    def _(part):
        spot = pl.multiple_of(part * lanes, lanes)
        taps = [
            jnp.broadcast_to(taps_ref[pl.ds(t, 1), pl.ds(spot, lanes)], (octet, lanes))
            for t in range(tap_count)
        ]
        past = tap_count - 1

        def frames_of(ref, begin):
            places = [spot + frame * length for frame in range(begin, frame_block)]
            return [
                ref[:, pl.ds(pl.multiple_of(place, lanes), lanes)].astype(f32) for place in places
            ]

        if history is None:
            window = frames_of(before_ref, frame_block - past)
        else:
            window = [history[part, j] for j in range(past)]
        window += frames_of(block_ref, 0)
        if history is not None:
            for j in range(past):
                history[part, j] = window[frame_block + j]

        def convolve(weights, values):
            sums = []
            for j in range(len(values) - len(weights) + 1):
                total = weights[-1] * values[j]
                for i in range(1, len(weights)):
                    total = total + weights[-1 - i] * values[j + i]
                sums.append(total)
            return sums

        even_taps, odd_taps = taps[past::-2], taps[past - 1 :: -2]
        odd = window[0::2]
        even = window[1::2]
        evens = convolve(even_taps, even)
        odds = convolve(odd_taps, odd)
        both_taps = [one + two for one, two in zip(even_taps, odd_taps)]
        both = convolve(both_taps, [one + two for one, two in zip(even, odd[1:])])
        for j in range(frame_block // 2):
            pair = (evens[j] + odds[j], both[j] - evens[j] - odds[j + 1])
            for frame, total in zip((2 * j, 2 * j + 1), pair):
                filtered[part, frame * octet : (frame + 1) * octet, :] = total

    kept = pl.ds(pl.multiple_of(step * frame_block, frame_block), frame_block)

    @pl.loop(0, octet)
    def _(antenna):
        for half in range(frame_block // octet):
            rows = pl.ds(half * octet * octet + antenna, octet, stride=octet)
            bins = real_transform([filtered[part, rows, :] for part in range(radix)])
            here = pl.ds(half * octet, octet)
            sections[0, here, :] = bins[0][0]
            sections[1, here, :] = bins[radix // 2][0]
            for k in range(1, radix // 2):
                sections[2 * k, here, :] = bins[k][0]
                sections[2 * k + 1, here, :] = bins[k][1]
        for group in range(radix // 2):
            for side in range(2):
                first, second = split_two(sections[2 * group + side])
                high[group, antenna, kept, side * lanes : (side + 1) * lanes] = first
                low[group, antenna, kept, side * lanes : (side + 1) * lanes] = second


def second_stage(high, low, wave_high, wave_low):
    dot = functools.partial(jnp.dot, preferred_element_type=f32)
    return dot(high, wave_high) + (dot(low, wave_high) + dot(high, wave_low))


def divisor(*sizes, most=3):
    return max(n for n in range(1, most + 1) if all(size % n == 0 for size in sizes))


def swap(one, two, width):
    lane = lax.broadcasted_iota(jnp.int32, (1, lanes), 1)
    even = lax.rem(lane // width, 2) == 0
    return (
        jnp.where(even, one, pltpu.roll(two, width, 1)),
        jnp.where(even, pltpu.roll(one, lanes - width, 1), two),
    )


def head_kernel(length, steps, each, size, skipped, with_edge, *refs):
    before_ref, block_ref, taps_ref, wave_high_ref, wave_low_ref = refs[:5]
    refs = refs[5:]
    if with_edge:
        edge_out, refs = refs[0], refs[1:]
    out_ref, refs = refs[0], refs[1:]
    filtered, sections, history, turned, high, low, wave_high, wave_low, done = refs
    step = pl.program_id(0)
    frames = high.shape[2]
    radix = length // lanes
    kept = lanes // 2
    taken = pl.ds(2 * skipped, 2 * size)
    waves = [
        pltpu.make_async_copy(wave_high_ref.at[taken], wave_high, done.at[1]),
        pltpu.make_async_copy(wave_low_ref.at[taken], wave_low, done.at[2]),
    ]
    edge = pltpu.make_async_copy(block_ref, edge_out, done.at[0]) if with_edge else None

    @pl.when(step == 0)
    def _():
        for copy in waves:
            copy.start()
        if steps > 1:
            past = history.shape[1]

            @pl.loop(0, radix, unroll=4)
            def _(part):
                for j in range(past):
                    place = part * lanes + (frame_block - past + j) * length
                    place = pl.ds(pl.multiple_of(place, lanes), lanes)
                    history[part, j] = before_ref[:, place].astype(f32)

    @pl.when(step < steps)
    def _():
        filter_frames(
            length,
            step,
            before_ref,
            block_ref,
            taps_ref,
            high,
            low,
            filtered,
            sections,
            history if steps > 1 else None,
        )

    if with_edge:

        @pl.when(step == steps - 1)
        def _():
            edge.start()

    @pl.when(step == steps)
    def _():
        for copy in waves:
            copy.wait()

    @pl.when(step >= steps)
    def _():
        rows = (octet * frames, 2 * lanes)
        totals = []
        for j in range(2 * each):
            at = (step - steps) * 2 * each + j
            pair = high[2 * skipped + at].reshape(rows), low[2 * skipped + at].reshape(rows)
            totals.append(second_stage(*pair, wave_high[at], wave_low[at]))
        for j in range(each):
            for block in range(steps):
                for a in range(0, octet, 2):
                    piece = []
                    for at in (a, a + 1):
                        begin = at * frames + block * frame_block
                        for total in totals[2 * j : 2 * j + 2]:
                            part = total[begin : begin + frame_block]
                            piece += [part[:, :lanes], part[:, lanes:]]
                    piece = jnp.concatenate(piece, axis=0).T
                    one, two = swap(piece[:kept], piece[kept:], kept)
                    turned[j * steps + block, pl.ds(a, kept, stride=octet), :] = one
                    turned[j * steps + block, pl.ds(a + 1, kept, stride=octet), :] = two
        for j in range(each * steps):
            out_ref[:, j] = turned[j].reshape(kept, octet, lanes).astype(bf16)

    if with_edge:

        @pl.when(step == pl.num_programs(0) - 1)
        def _():
            edge.wait()


def head(before, before_block, samples, taps, tables, first, steps, skipped, size, with_edge):
    length = taps.shape[1]
    radix = length // lanes
    groups = radix // 2
    kept = lanes // 2
    frames = steps * frame_block
    width = frame_block * length
    each = divisor(size, skipped, most=4 if steps == 1 else 2)
    anywhere = pl.BlockSpec(memory_space=pl.ANY)
    out_shape, out_specs = [], []
    if with_edge:
        out_shape.append(jax.ShapeDtypeStruct((octet, width), bf16))
        out_specs.append(anywhere)
    out_shape.append(jax.ShapeDtypeStruct((kept, size * steps, octet, lanes), bf16))
    out_specs.append(
        pl.BlockSpec(
            (kept, each * steps, octet, lanes), lambda i: (0, jnp.maximum(i - steps, 0), 0, 0)
        )
    )
    return pl.pallas_call(
        functools.partial(head_kernel, length, steps, each, size, skipped, with_edge),
        grid=(steps + size // each,),
        in_specs=[
            pl.BlockSpec((octet, width), lambda i: (0, before_block)),
            pl.BlockSpec((octet, width), lambda i: (0, first + jnp.minimum(i, steps - 1))),
            pl.BlockSpec(taps.shape, lambda i: (0, 0)),
            anywhere,
            anywhere,
        ],
        out_specs=out_specs,
        out_shape=out_shape,
        scratch_shapes=[
            pltpu.VMEM((radix, frame_block * octet, lanes), f32),
            pltpu.VMEM((radix, frame_block, lanes), f32),
            pltpu.VMEM((radix, taps.shape[0] - 1, octet, lanes), f32),
            pltpu.VMEM((each * steps, kept * octet, lanes), f32),
            pltpu.VMEM((groups, octet, frames, 2 * lanes), bf16),
            pltpu.VMEM((groups, octet, frames, 2 * lanes), bf16),
            pltpu.VMEM((2 * size, 2 * lanes, 2 * lanes), bf16),
            pltpu.VMEM((2 * size, 2 * lanes, 2 * lanes), bf16),
            pltpu.SemaphoreType.DMA((3,)),
        ],
        compiler_params=pltpu.CompilerParams(vmem_limit_bytes=later_vmem if skipped else head_vmem),
        cost_estimate=pl.CostEstimate(
            flops=steps * 1_000_000_000, bytes_accessed=steps * 1_000_000, transcendentals=0
        ),
        name="head",
    )(before, samples, taps, *tables)


def phase_tables(length):
    radix = length // lanes
    kept = lanes // 2
    q = np.arange(lanes)
    m = np.arange(kept)

    def waves(k):
        angle = 2 * np.pi * (np.outer(q, k + radix * m) % length) / length
        return np.cos(angle), np.sin(angle)

    zero = np.zeros((lanes, kept))
    (c, s), (oc, os) = waves(0), waves(radix // 2)
    tables = [np.block([[c, zero, -s, zero], [zero, oc, zero, -os]])]
    for k in range(1, radix // 2):
        (c, s), (oc, os) = waves(k), waves(radix - k)
        tables.append(np.block([[c, oc, -s, -os], [s, -os, c, -oc]]))
    tables = np.stack(tables).astype(np.float32)
    high = tables.astype(ml_dtypes.bfloat16)
    low = (tables - high.astype(np.float32)).astype(ml_dtypes.bfloat16)
    return high, low


def contract_last(left, right):
    return lax.dot_general(left, right, (((1,), (1,)), ((), ())), preferred_element_type=f32)


def covariance_kernel(place, scale, widths, *refs):
    x_refs, q_ref = refs[: len(widths)], refs[len(widths)]
    packed = len(widths) > 1
    out_ref, ready, done = refs[-3:]
    step = pl.program_id(0)
    steps = pl.num_programs(0)
    slot = lax.rem(step, 2)
    octets, shards = x_refs[0].shape[:2]
    antennas = octets * octet
    columns = x_refs[0].shape[2] // widths[0]
    count = columns * (4 if packed else 1)

    def copies(at, which):
        return [
            pltpu.make_async_copy(
                ready.at[which, j], out_ref.at[place(at * count + j)], done.at[which, j]
            )
            for j in range(count)
        ]

    @pl.when(step >= 2)
    def _():
        for copy in copies(step - 2, slot):
            copy.wait()

    def load(ref, t, j):
        if t >= shards:
            return jnp.zeros((antennas, lanes), f32)
        return ref[:, t, j].astype(f32).reshape(antennas, lanes)

    def channels(j):
        parts = [[] for _ in range(8 if packed else 2)]
        for t in range(0, shards, 2):
            tiles = [
                load(ref, u, j * width + at)
                for u in (t, t + 1)
                for ref, width in zip(x_refs, widths)
                for at in range(width)
            ]
            stride = len(tiles) // 2
            while stride:
                for low in range(len(tiles)):
                    if not low & stride:
                        tiles[low], tiles[low + stride] = swap(
                            tiles[low], tiles[low + stride], lanes * stride // len(tiles)
                        )
                stride //= 2
            for part, tile in zip(parts, tiles):
                part.append(tile)
        return [
            jnp.concatenate(real + imag, axis=1) for real, imag in zip(parts[0::2], parts[1::2])
        ]

    def turned(v):
        middle = v.shape[1] // 2
        return jnp.concatenate([v[:, middle:], -v[:, :middle]], axis=1)

    xs = [x for j in range(columns) for x in channels(j)]
    qs = [split_three(q_ref[place(step * count + at)]) for at in range(count)]
    zs = []
    for x, (qh, qm, ql) in zip(xs, qs):
        left = jnp.concatenate([qh, qm, ql, jnp.zeros_like(qh)], axis=0).astype(bf16)
        z = jnp.dot(left, x.astype(bf16), preferred_element_type=f32)
        zs.append(split_three(z[:octet] + z[octet : 2 * octet] + z[2 * octet : 3 * octet]))
    parts = []
    for x, (qh, qm, ql), (zh, zm, zl) in zip(xs, qs, zs):
        left = jnp.concatenate([qh, qh, qm, qm, qh, ql], axis=0).astype(bf16)
        right = jnp.concatenate([zh, zm, zh, zm, zl, zh], axis=0).astype(bf16)
        taken = lax.dot_general(left, right, (((0,), (0,)), ((), ())), preferred_element_type=f32)
        parts.append(split_two(x - taken))
    for at, ((high, low), copy) in enumerate(zip(parts, copies(step, slot))):
        left = jnp.concatenate([high, turned(high)], axis=0)
        total = contract_last(left, jnp.concatenate([high, low], axis=0))
        same, cross = total[:, :antennas], total[:, antennas:]
        real, imag = cross[:antennas], cross[antennas:]
        cross = jnp.concatenate([real + real.T, imag - imag.T], axis=0)
        total = (same + cross) * scale
        ready[slot, at] = total.reshape(2, antennas, antennas)
        copy.start()

    @pl.when(step == steps - 1)
    def _():
        @pl.when(step >= 1)
        def _():
            for copy in copies(step - 1, 1 - slot):
                copy.wait()

        for copy in copies(step, slot):
            copy.wait()


def covariances(received, basis, place, frame_total, total, previous, last):
    array, runs, _, taken, _ = received[0]
    octets, shards = array.shape[:2]
    antennas = octets * octet
    widths = [one[4] for one in received]
    sizes = [n for a, r, begin, _, width in received for n in (a.shape[2] // (r * width), begin)]
    packed = len(received) > 1
    each = divisor(taken, *sizes, most=2 if packed else 8)
    count = each * (4 if packed else 1)
    steps = taken // each

    def window(array, runs, begin, _, width):
        stride = array.shape[2] // (runs * width * each)

        def index(i):
            run = i // steps
            return (0, 0, run * stride + begin // each + i - run * steps, 0, 0)

        return pl.BlockSpec((octets, shards, each * width, octet, lanes), index)

    in_specs = [window(*one) for one in received]
    in_specs.append(pl.BlockSpec(basis.shape, lambda i: (0, 0, 0)))
    operands = [*(one[0] for one in received), basis]
    aliases = {}
    if previous is not None:
        in_specs.append(pl.BlockSpec(memory_space=pl.ANY))
        aliases = {len(operands): 0}
        operands.append(previous)
    return pl.pallas_call(
        functools.partial(covariance_kernel, place, 1.0 / frame_total, widths),
        grid=(runs * steps,),
        in_specs=in_specs,
        out_specs=pl.BlockSpec(memory_space=pl.ANY),
        out_shape=jax.ShapeDtypeStruct((total, 2, antennas, antennas), f32),
        scratch_shapes=[
            pltpu.VMEM((2, count, 2, antennas, antennas), f32),
            pltpu.SemaphoreType.DMA((2, count)),
        ],
        input_output_aliases=aliases,
        compiler_params=pltpu.CompilerParams(vmem_limit_bytes=last_vmem if last else covariance_vmem),
        cost_estimate=pl.CostEstimate(
            flops=runs * steps * count * 200_000_000,
            bytes_accessed=runs * steps * count * 200_000,
            transcendentals=0,
        ),
        name="covariances",
    )(*operands)


def orthonormal(vectors):
    found = []
    for column in range(vectors.shape[1]):
        residue = vectors[:, column, :]
        for earlier in found:
            residue = residue - earlier * jnp.sum(earlier * residue, axis=-1, keepdims=True)
        found.append(
            residue / jnp.sqrt(jnp.sum(residue * residue, axis=-1, keepdims=True) + epsilon)
        )
    return jnp.stack(found, axis=1)


def basis_of(chosen, counted, steering):
    count, slots = chosen.shape
    directions = steering.shape[0]
    onehot = (
        chosen[:, :, None] == lax.broadcasted_iota(jnp.int32, (count, slots, directions), 2)
    ).astype(f32)
    live = (lax.broadcasted_iota(jnp.int32, (count, slots), 1) < counted[:, None]).astype(f32)
    vectors = jnp.einsum("crn,na->cra", onehot, steering, precision=highest) * live[:, :, None]
    basis = orthonormal(vectors)
    return jnp.pad(basis, ((0, 0), (0, octet - slots), (0, 0)))


def per_device(samples, taps, steering, interferer_ids, ranks):
    antennas, width = samples.shape
    length = taps.shape[1]
    frames = width // length
    radix = length // lanes
    groups = radix // 2
    kept = lanes // 2
    shards = lax.axis_size("tm")
    spread = lax.axis_size("chan")
    devices = spread * shards
    owned = interferer_ids.shape[0]
    frame_total = frames * shards

    padded = samples
    if antennas < octet:
        padded = jnp.pad(samples, ((0, octet - antennas), (0, 0)))
    tables = [jnp.asarray(table) for table in phase_tables(length)]
    blocks = frames // frame_block
    whole_runs = owned % radix == 0
    runs = owned // radix
    twos = groups // 2
    cuts = (twos - last_twos, last_twos) if whole_runs else (twos,)

    def exchange(spectra):
        received = lax.all_to_all(spectra, ("chan", "tm"), split_axis=0, concat_axis=0, tiled=True)
        received = received.reshape(spread, shards, -1, antennas, lanes)
        if antennas < octet:
            received = received.transpose(1, 2, 0, 3, 4).reshape(
                shards, -1, spread * antennas // octet, octet, lanes
            ).transpose(2, 0, 1, 3, 4)
        return received

    def channel_at(first, count):
        def place(index):
            run = index // (4 * count)
            two = (index - run * (4 * count)) // 4
            group = 2 * (first + two) + index % 2
            mirrored = jnp.where(group == 0, groups, radix - group)
            return run * radix + jnp.where(index % 4 < 2, group, mirrored)

        return place

    edge, early = head(padded, blocks - 2, padded, taps, tables, blocks - 1, 1, 0, twos, True)
    before = lax.ppermute(edge, "tm", [(i, i + 1) for i in range(shards - 1)])
    if whole_runs:
        arrived = exchange(early.reshape(devices, -1, octet, lanes))
    basis = basis_of(interferer_ids, ranks, steering)

    def later(first, count):
        return head(before, 0, padded, taps, tables, 0, blocks - 1, first, count, False)[0]

    out = None
    if whole_runs:
        first = 0
        pieces = []
        for count in cuts:
            if first:
                before, basis = lax.optimization_barrier((before, basis))
            sent = later(first, count).reshape(devices, -1, octet, lanes)
            if not first:
                sent, arrived = lax.optimization_barrier((sent, arrived))
            pieces.append((exchange(sent), first, count))
            first += count
        for received, first, count in pieces:
            parts = (
                (received, runs, 0, count, blocks - 1),
                (arrived, runs, first, count, 1),
            )
            out = covariances(
                parts, basis, channel_at(first, count), frame_total, owned, out, first > 0
            )
    else:
        tiles = jnp.concatenate(
            [
                later(0, twos).reshape(kept, twos, blocks - 1, octet, 4, 2, frame_block),
                early.reshape(kept, twos, 1, octet, 4, 2, frame_block),
            ],
            axis=2,
        )
        tiles = tiles.transpose(0, 1, 4, 3, 5, 2, 6).reshape(kept, radix, octet, lanes)
        order = [
            k
            for g in range(0, groups, 2)
            for k in (g, g + 1, radix - g if g else groups, radix - g - 1)
        ]
        tiles = tiles[:, np.argsort(order), :antennas].reshape(devices, owned, antennas, lanes)
        received = exchange(tiles)
        parts = ((received, 1, 0, owned, 1),)
        out = covariances(parts, basis, lambda index: index, frame_total, owned, None, True)
    return out


last_twos = 2
head_vmem = 56 * 1024 * 1024
later_vmem = 32 * 1024 * 1024
covariance_vmem = 24 * 1024 * 1024
last_vmem = 24 * 1024 * 1024


def solution(mesh):
    in_specs = (P("chan", "tm"), P(), P(), P(("chan", "tm"), None), P(("chan", "tm")))
    out_specs = P(("chan", "tm"), None, None, None)
    return jax.shard_map(
        per_device, mesh=mesh, in_specs=in_specs, out_specs=out_specs, check_vma=False
    )
```

```python
import functools
import math

import jax
import jax.numpy as jnp
import ml_dtypes
import numpy as np
from jax import lax
from jax.experimental import pallas as pl
from jax.experimental.pallas import tpu as pltpu
from jax.sharding import PartitionSpec as P

lanes = 128
octet = 8
frame_block = 16
epsilon = 1e-06
highest = lax.Precision.HIGHEST
f32 = jnp.float32
bf16 = jnp.bfloat16


def real_transform(x):
    size = len(x)
    if size == 2:
        return [(x[0] + x[1], None), (x[0] - x[1], None)]
    even = real_transform(x[0::2])
    odd = real_transform(x[1::2])
    half = size // 2
    bins = [None] * (half + 1)
    bins[0] = (even[0][0] + odd[0][0], None)
    bins[half] = (even[0][0] - odd[0][0], None)
    bins[half // 2] = (even[half // 2][0], -odd[half // 2][0])
    for k in range(1, half // 2):
        er, ei = even[k]
        o_r, oi = odd[k]
        c = math.cos(2 * math.pi * k / size)
        s = math.sin(2 * math.pi * k / size)
        if 4 * k == half:
            tr = (o_r + oi) * c
            ti = (oi - o_r) * c
        else:
            tr = o_r * c + oi * s
            ti = oi * c - o_r * s
        bins[k] = (er + tr, ei + ti)
        bins[half - k] = (er - tr, ti - ei)
    return bins


def split_two(x):
    high = x.astype(bf16)
    low = (x - high.astype(f32)).astype(bf16)
    return high, low


def split_three(x):
    high = x.astype(bf16).astype(f32)
    rest = x - high
    middle = rest.astype(bf16).astype(f32)
    return high, middle, rest - middle


def filter_frames(length, step, before_ref, block_ref, taps_ref, high, low, filtered, sections, history):
    tap_count = taps_ref.shape[0]
    radix = length // lanes

    @pl.loop(0, radix, unroll=2)
    def _(part):
        spot = pl.multiple_of(part * lanes, lanes)
        taps = [
            jnp.broadcast_to(taps_ref[pl.ds(t, 1), pl.ds(spot, lanes)], (octet, lanes))
            for t in range(tap_count)
        ]
        past = tap_count - 1

        def frames_of(ref, begin):
            places = [spot + frame * length for frame in range(begin, frame_block)]
            return [
                ref[:, pl.ds(pl.multiple_of(place, lanes), lanes)].astype(f32) for place in places
            ]

        if history is None:
            window = frames_of(before_ref, frame_block - past)
        else:
            window = [history[part, j] for j in range(past)]
        window += frames_of(block_ref, 0)
        if history is not None:
            for j in range(past):
                history[part, j] = window[frame_block + j]

        def convolve(weights, values):
            sums = []
            for j in range(len(values) - len(weights) + 1):
                total = weights[-1] * values[j]
                for i in range(1, len(weights)):
                    total = total + weights[-1 - i] * values[j + i]
                sums.append(total)
            return sums

        even_taps, odd_taps = taps[past::-2], taps[past - 1 :: -2]
        odd = window[0::2]
        even = window[1::2]
        evens = convolve(even_taps, even)
        odds = convolve(odd_taps, odd)
        both_taps = [one + two for one, two in zip(even_taps, odd_taps)]
        both = convolve(both_taps, [one + two for one, two in zip(even, odd[1:])])
        for j in range(frame_block // 2):
            pair = (evens[j] + odds[j], both[j] - evens[j] - odds[j + 1])
            for frame, total in zip((2 * j, 2 * j + 1), pair):
                filtered[part, pl.ds(frame, octet, stride=frame_block), :] = total

    kept = pl.ds(pl.multiple_of(step * frame_block, frame_block), frame_block)

    @pl.loop(0, octet)
    def _(antenna):
        for half in range(frame_block // octet):
            rows = pl.ds(pl.multiple_of(antenna * frame_block + half * octet, octet), octet)
            bins = real_transform([filtered[part, rows, :] for part in range(radix)])
            here = pl.ds(half * octet, octet)
            sections[0, here, :] = bins[0][0]
            sections[1, here, :] = bins[radix // 2][0]
            for k in range(1, radix // 2):
                sections[2 * k, here, :] = bins[k][0]
                sections[2 * k + 1, here, :] = bins[k][1]
        for group in range(radix // 2):
            for side in range(2):
                first, second = split_two(sections[2 * group + side])
                high[group, antenna, kept, side * lanes : (side + 1) * lanes] = first
                low[group, antenna, kept, side * lanes : (side + 1) * lanes] = second


def second_stage(high, low, wave_high, wave_low):
    dot = functools.partial(jnp.dot, preferred_element_type=f32)
    return dot(high, wave_high) + (dot(low, wave_high) + dot(high, wave_low))


def divisor(*sizes, most=3):
    return max(n for n in range(1, most + 1) if all(size % n == 0 for size in sizes))


def swap(one, two, width):
    lane = lax.broadcasted_iota(jnp.int32, (1, lanes), 1)
    even = lax.rem(lane // width, 2) == 0
    return (
        jnp.where(even, one, pltpu.roll(two, width, 1)),
        jnp.where(even, pltpu.roll(one, lanes - width, 1), two),
    )


def head_kernel(length, steps, each, size, skipped, *refs):
    before_ref, block_ref, taps_ref, wave_high_ref, wave_low_ref = refs[:5]
    out_ref, *refs = refs[5:]
    filtered, sections, history, turned, high, low, wave_high, wave_low, done = refs
    step = pl.program_id(0)
    frames = high.shape[2]
    radix = length // lanes
    kept = lanes // 2
    taken = pl.ds(2 * skipped, 2 * size)
    waves = [
        pltpu.make_async_copy(wave_high_ref.at[taken], wave_high, done.at[0]),
        pltpu.make_async_copy(wave_low_ref.at[taken], wave_low, done.at[1]),
    ]

    @pl.when(step == 0)
    def _():
        for copy in waves:
            copy.start()
        if steps > 1:
            past = history.shape[1]

            @pl.loop(0, radix, unroll=4)
            def _(part):
                for j in range(past):
                    place = part * lanes + (frame_block - past + j) * length
                    place = pl.ds(pl.multiple_of(place, lanes), lanes)
                    history[part, j] = before_ref[:, place].astype(f32)

    @pl.when(step < steps)
    def _():
        filter_frames(
            length,
            step,
            before_ref,
            block_ref,
            taps_ref,
            high,
            low,
            filtered,
            sections,
            history if steps > 1 else None,
        )

    @pl.when(step == steps)
    def _():
        for copy in waves:
            copy.wait()

    @pl.when(step >= steps)
    def _():
        rows = (octet * frames, 2 * lanes)
        totals = []
        for j in range(2 * each):
            at = (step - steps) * 2 * each + j
            pair = high[2 * skipped + at].reshape(rows), low[2 * skipped + at].reshape(rows)
            totals.append(second_stage(*pair, wave_high[at], wave_low[at]))
        for j in range(each):
            for block in range(steps):
                for a in range(0, octet, 2):
                    piece = []
                    for at in (a, a + 1):
                        begin = at * frames + block * frame_block
                        for total in totals[2 * j : 2 * j + 2]:
                            part = total[begin : begin + frame_block]
                            piece += [part[:, :lanes], part[:, lanes:]]
                    piece = jnp.concatenate(piece, axis=0).T
                    one, two = swap(piece[:kept], piece[kept:], kept)
                    turned[j * steps + block, pl.ds(a, kept, stride=octet), :] = one
                    turned[j * steps + block, pl.ds(a + 1, kept, stride=octet), :] = two
        for j in range(each * steps):
            out_ref[:, j] = turned[j].reshape(kept, octet, lanes).astype(bf16)


def head(before, before_block, samples, taps, tables, first, steps, skipped, size):
    length = taps.shape[1]
    radix = length // lanes
    groups = radix // 2
    kept = lanes // 2
    frames = steps * frame_block
    width = frame_block * length
    each = divisor(size, skipped, most=4 if steps == 1 else 2)
    anywhere = pl.BlockSpec(memory_space=pl.ANY)
    return pl.pallas_call(
        functools.partial(head_kernel, length, steps, each, size, skipped),
        grid=(steps + size // each,),
        in_specs=[
            pl.BlockSpec((octet, width), lambda i: (0, before_block)),
            pl.BlockSpec((octet, width), lambda i: (0, first + jnp.minimum(i, steps - 1))),
            pl.BlockSpec(taps.shape, lambda i: (0, 0)),
            anywhere,
            anywhere,
        ],
        out_specs=pl.BlockSpec(
            (kept, each * steps, octet, lanes), lambda i: (0, jnp.maximum(i - steps, 0), 0, 0)
        ),
        out_shape=jax.ShapeDtypeStruct((kept, size * steps, octet, lanes), bf16),
        scratch_shapes=[
            pltpu.VMEM((radix, frame_block * octet, lanes), f32),
            pltpu.VMEM((radix, frame_block, lanes), f32),
            pltpu.VMEM((radix, taps.shape[0] - 1, octet, lanes), f32),
            pltpu.VMEM((each * steps, kept * octet, lanes), f32),
            pltpu.VMEM((groups, octet, frames, 2 * lanes), bf16),
            pltpu.VMEM((groups, octet, frames, 2 * lanes), bf16),
            pltpu.VMEM((2 * size, 2 * lanes, 2 * lanes), bf16),
            pltpu.VMEM((2 * size, 2 * lanes, 2 * lanes), bf16),
            pltpu.SemaphoreType.DMA((2,)),
        ],
        compiler_params=pltpu.CompilerParams(vmem_limit_bytes=later_vmem if skipped else head_vmem),
        cost_estimate=pl.CostEstimate(
            flops=steps * 1_000_000_000, bytes_accessed=steps * 1_000_000, transcendentals=0
        ),
        name="head",
    )(before, samples, taps, *tables)


def phase_tables(length):
    radix = length // lanes
    kept = lanes // 2
    q = np.arange(lanes)
    m = np.arange(kept)

    def waves(k):
        angle = 2 * np.pi * (np.outer(q, k + radix * m) % length) / length
        return np.cos(angle), np.sin(angle)

    zero = np.zeros((lanes, kept))
    (c, s), (oc, os) = waves(0), waves(radix // 2)
    tables = [np.block([[c, zero, -s, zero], [zero, oc, zero, -os]])]
    for k in range(1, radix // 2):
        (c, s), (oc, os) = waves(k), waves(radix - k)
        tables.append(np.block([[c, oc, -s, -os], [s, -os, c, -oc]]))
    tables = np.stack(tables).astype(np.float32)
    high = tables.astype(ml_dtypes.bfloat16)
    low = (tables - high.astype(np.float32)).astype(ml_dtypes.bfloat16)
    return high, low


def contract_last(left, right):
    return lax.dot_general(left, right, (((1,), (1,)), ((), ())), preferred_element_type=f32)


def covariance_kernel(place, scale, widths, *refs):
    x_refs, q_ref = refs[: len(widths)], refs[len(widths)]
    packed = len(widths) > 1
    out_ref, ready, done = refs[-3:]
    step = pl.program_id(0)
    steps = pl.num_programs(0)
    slot = lax.rem(step, 2)
    octets, shards, runs = x_refs[0].shape[:3]
    antennas = octets * octet
    columns = x_refs[0].shape[3] // widths[0]
    held = [
        (run, j, c) for run in range(runs) for j in range(columns) for c in range(4 if packed else 1)
    ]
    count = len(held)

    def target(at, index):
        run, j, c = held[index]
        return place(run, at * columns + j, c)

    def copies(at, which):
        return [
            pltpu.make_async_copy(
                ready.at[which, j], out_ref.at[target(at, j)], done.at[which, j]
            )
            for j in range(count)
        ]

    @pl.when(step >= 2)
    def _():
        for copy in copies(step - 2, slot):
            copy.wait()

    def load(ref, t, run, j):
        if t >= shards:
            return jnp.zeros((antennas, lanes), f32)
        return ref[:, t, run, j].astype(f32).reshape(antennas, lanes)

    def channels(run, j):
        parts = [[] for _ in range(8 if packed else 2)]
        for t in range(0, shards, 2):
            tiles = [
                load(ref, u, run, j * width + at)
                for u in (t, t + 1)
                for ref, width in zip(x_refs, widths)
                for at in range(width)
            ]
            stride = len(tiles) // 2
            while stride:
                for low in range(len(tiles)):
                    if not low & stride:
                        tiles[low], tiles[low + stride] = swap(
                            tiles[low], tiles[low + stride], lanes * stride // len(tiles)
                        )
                stride //= 2
            for part, tile in zip(parts, tiles):
                part.append(tile)
        return [
            jnp.concatenate(real + imag, axis=1) for real, imag in zip(parts[0::2], parts[1::2])
        ]

    def turned(v):
        middle = v.shape[1] // 2
        return jnp.concatenate([v[:, middle:], -v[:, :middle]], axis=1)

    xs = [x for run in range(runs) for j in range(columns) for x in channels(run, j)]
    qs = [split_three(q_ref[target(step, at)]) for at in range(count)]
    zs = []
    for x, (qh, qm, ql) in zip(xs, qs):
        left = jnp.concatenate([qh, qm, ql, jnp.zeros_like(qh)], axis=0).astype(bf16)
        z = jnp.dot(left, x.astype(bf16), preferred_element_type=f32)
        zs.append(split_three(z[:octet] + z[octet : 2 * octet] + z[2 * octet : 3 * octet]))
    parts = []
    for x, (qh, qm, ql), (zh, zm, zl) in zip(xs, qs, zs):
        left = jnp.concatenate([qh, qh, qm, qm, qh, ql], axis=0).astype(bf16)
        right = jnp.concatenate([zh, zm, zh, zm, zl, zh], axis=0).astype(bf16)
        taken = lax.dot_general(left, right, (((0,), (0,)), ((), ())), preferred_element_type=f32)
        parts.append(split_two(x - taken))
    for at, ((high, low), copy) in enumerate(zip(parts, copies(step, slot))):
        left = jnp.concatenate([high, turned(high)], axis=0)
        total = contract_last(left, jnp.concatenate([high, low], axis=0))
        same, cross = total[:, :antennas], total[:, antennas:]
        real, imag = cross[:antennas], cross[antennas:]
        cross = jnp.concatenate([real + real.T, imag - imag.T], axis=0)
        total = (same + cross) * scale
        ready[slot, at] = total.reshape(2, antennas, antennas)
        copy.start()

    @pl.when(step == steps - 1)
    def _():
        @pl.when(step >= 1)
        def _():
            for copy in copies(step - 1, 1 - slot):
                copy.wait()

        for copy in copies(step, slot):
            copy.wait()


def covariances(received, basis, place, frame_total, total, previous, last):
    array, runs, _, taken, _ = received[0]
    octets, shards = array.shape[:2]
    antennas = octets * octet
    widths = [one[4] for one in received]
    packed = len(received) > 1
    sizes = [begin for _, _, begin, _, _ in received]
    each = divisor(taken, *sizes, most=max(1, 4 // runs) if packed else 8)
    count = runs * each * (4 if packed else 1)
    steps = taken // each

    def window(begin, width):
        return pl.BlockSpec(
            (octets, shards, runs, each * width, octet, lanes),
            lambda i: (0, 0, 0, begin // each + i, 0, 0),
        )

    in_specs = [window(begin, width) for _, _, begin, _, width in received]
    in_specs.append(pl.BlockSpec(basis.shape, lambda i: (0, 0, 0)))
    operands = [one[0].reshape(octets, shards, runs, -1, octet, lanes) for one in received]
    operands.append(basis)
    aliases = {}
    if previous is not None:
        in_specs.append(pl.BlockSpec(memory_space=pl.ANY))
        aliases = {len(operands): 0}
        operands.append(previous)
    return pl.pallas_call(
        functools.partial(covariance_kernel, place, 1.0 / frame_total, widths),
        grid=(steps,),
        in_specs=in_specs,
        out_specs=pl.BlockSpec(memory_space=pl.ANY),
        out_shape=jax.ShapeDtypeStruct((total, 2, antennas, antennas), f32),
        scratch_shapes=[
            pltpu.VMEM((2, count, 2, antennas, antennas), f32),
            pltpu.SemaphoreType.DMA((2, count)),
        ],
        input_output_aliases=aliases,
        compiler_params=pltpu.CompilerParams(vmem_limit_bytes=last_vmem if last else covariance_vmem),
        cost_estimate=pl.CostEstimate(
            flops=steps * count * 200_000_000,
            bytes_accessed=steps * count * 200_000,
            transcendentals=0,
        ),
        name="covariances",
    )(*operands)


def orthonormal(vectors):
    found = []
    for column in range(vectors.shape[1]):
        residue = vectors[:, column, :]
        for earlier in found:
            residue = residue - earlier * jnp.sum(earlier * residue, axis=-1, keepdims=True)
        found.append(
            residue / jnp.sqrt(jnp.sum(residue * residue, axis=-1, keepdims=True) + epsilon)
        )
    return jnp.stack(found, axis=1)


def basis_of(chosen, counted, steering):
    count, slots = chosen.shape
    directions = steering.shape[0]
    onehot = (
        chosen[:, :, None] == lax.broadcasted_iota(jnp.int32, (count, slots, directions), 2)
    ).astype(f32)
    live = (lax.broadcasted_iota(jnp.int32, (count, slots), 1) < counted[:, None]).astype(f32)
    vectors = jnp.einsum("crn,na->cra", onehot, steering, precision=highest) * live[:, :, None]
    basis = orthonormal(vectors)
    return jnp.pad(basis, ((0, 0), (0, octet - slots), (0, 0)))


def per_device(samples, taps, steering, interferer_ids, ranks):
    antennas, width = samples.shape
    length = taps.shape[1]
    frames = width // length
    radix = length // lanes
    groups = radix // 2
    kept = lanes // 2
    shards = lax.axis_size("tm")
    spread = lax.axis_size("chan")
    devices = spread * shards
    owned = interferer_ids.shape[0]
    frame_total = frames * shards

    padded = samples
    if antennas < octet:
        padded = jnp.pad(samples, ((0, octet - antennas), (0, 0)))
    tables = [jnp.asarray(table) for table in phase_tables(length)]
    blocks = frames // frame_block
    whole_runs = owned % radix == 0
    runs = owned // radix
    twos = groups // 2
    cuts = (twos - last_twos, last_twos) if whole_runs else (twos,)

    def exchange(spectra):
        received = lax.all_to_all(spectra, ("chan", "tm"), split_axis=0, concat_axis=0, tiled=True)
        received = received.reshape(spread, shards, -1, antennas, lanes)
        if antennas < octet:
            received = received.transpose(1, 2, 0, 3, 4).reshape(
                shards, -1, spread * antennas // octet, octet, lanes
            ).transpose(2, 0, 1, 3, 4)
        return received

    def channel_at(first):
        def place(run, column, c):
            group = 2 * (first + column) + c % 2
            mirrored = jnp.where(group == 0, groups, radix - group)
            return run * radix + (group if c < 2 else mirrored)

        return place

    early = head(padded, blocks - 2, padded, taps, tables, blocks - 1, 1, 0, twos)
    early, behind = lax.optimization_barrier((early, padded))
    edge = behind[:, width - frame_block * length :]
    before = lax.ppermute(edge, "tm", [(i, i + 1) for i in range(shards - 1)])
    if whole_runs:
        arrived = exchange(early.reshape(devices, -1, octet, lanes))
    basis = basis_of(interferer_ids, ranks, steering)

    def later(first, count):
        return head(before, 0, padded, taps, tables, 0, blocks - 1, first, count)

    out = None
    if whole_runs:
        first = 0
        pieces = []
        for count in cuts:
            if first:
                before, basis = lax.optimization_barrier((before, basis))
            sent = later(first, count).reshape(devices, -1, octet, lanes)
            if not first:
                sent, arrived = lax.optimization_barrier((sent, arrived))
            pieces.append((exchange(sent), first, count))
            first += count
        for received, first, count in pieces:
            parts = (
                (received, runs, 0, count, blocks - 1),
                (arrived, runs, first, count, 1),
            )
            out = covariances(
                parts, basis, channel_at(first), frame_total, owned, out, first > 0
            )
    else:
        tiles = jnp.concatenate(
            [
                later(0, twos).reshape(kept, twos, blocks - 1, octet, 4, 2, frame_block),
                early.reshape(kept, twos, 1, octet, 4, 2, frame_block),
            ],
            axis=2,
        )
        tiles = tiles.transpose(0, 1, 4, 3, 5, 2, 6).reshape(kept, radix, octet, lanes)
        order = [
            k
            for g in range(0, groups, 2)
            for k in (g, g + 1, radix - g if g else groups, radix - g - 1)
        ]
        tiles = tiles[:, np.argsort(order), :antennas].reshape(devices, owned, antennas, lanes)
        received = exchange(tiles)
        parts = ((received, 1, 0, owned, 1),)
        out = covariances(parts, basis, lambda run, column, c: column, frame_total, owned, None, True)
    return out


last_twos = 2
head_vmem = 56 * 1024 * 1024
later_vmem = 32 * 1024 * 1024
covariance_vmem = 24 * 1024 * 1024
last_vmem = 24 * 1024 * 1024


def solution(mesh):
    in_specs = (P("chan", "tm"), P(), P(), P(("chan", "tm"), None), P(("chan", "tm")))
    out_specs = P(("chan", "tm"), None, None, None)
    return jax.shard_map(
        per_device, mesh=mesh, in_specs=in_specs, out_specs=out_specs, check_vma=False
    )
```

```python
import functools
import math

import jax
import jax.numpy as jnp
import ml_dtypes
import numpy as np
from jax import lax
from jax.experimental import pallas as pl
from jax.experimental.pallas import tpu as pltpu
from jax.sharding import PartitionSpec as P

lanes = 128
octet = 8
frame_block = 16
epsilon = 1e-06
highest = lax.Precision.HIGHEST
f32 = jnp.float32
bf16 = jnp.bfloat16


def real_transform(x):
    size = len(x)
    if size == 2:
        return [(x[0] + x[1], None), (x[0] - x[1], None)]
    even = real_transform(x[0::2])
    odd = real_transform(x[1::2])
    half = size // 2
    bins = [None] * (half + 1)
    bins[0] = (even[0][0] + odd[0][0], None)
    bins[half] = (even[0][0] - odd[0][0], None)
    bins[half // 2] = (even[half // 2][0], -odd[half // 2][0])
    for k in range(1, half // 2):
        er, ei = even[k]
        o_r, oi = odd[k]
        c = math.cos(2 * math.pi * k / size)
        s = math.sin(2 * math.pi * k / size)
        if 4 * k == half:
            tr = (o_r + oi) * c
            ti = (oi - o_r) * c
        else:
            tr = o_r * c + oi * s
            ti = oi * c - o_r * s
        bins[k] = (er + tr, ei + ti)
        bins[half - k] = (er - tr, ti - ei)
    return bins


def split_two(x):
    high = x.astype(bf16)
    low = (x - high.astype(f32)).astype(bf16)
    return high, low


def split_three(x):
    high = x.astype(bf16).astype(f32)
    rest = x - high
    middle = rest.astype(bf16).astype(f32)
    return high, middle, rest - middle


def filter_frames(length, step, before_ref, block_ref, taps_ref, high, low, filtered, sections, history):
    tap_count = taps_ref.shape[0]
    radix = length // lanes

    @pl.loop(0, radix, unroll=2)
    def _(part):
        spot = pl.multiple_of(part * lanes, lanes)
        taps = [
            jnp.broadcast_to(taps_ref[pl.ds(t, 1), pl.ds(spot, lanes)], (octet, lanes))
            for t in range(tap_count)
        ]
        past = tap_count - 1

        def frames_of(ref, begin):
            places = [spot + frame * length for frame in range(begin, frame_block)]
            return [
                ref[:, pl.ds(pl.multiple_of(place, lanes), lanes)].astype(f32) for place in places
            ]

        if history is None:
            window = frames_of(before_ref, frame_block - past)
        else:
            window = [history[part, j] for j in range(past)]
        window += frames_of(block_ref, 0)
        if history is not None:
            for j in range(past):
                history[part, j] = window[frame_block + j]

        def convolve(weights, values):
            sums = []
            for j in range(len(values) - len(weights) + 1):
                total = weights[-1] * values[j]
                for i in range(1, len(weights)):
                    total = total + weights[-1 - i] * values[j + i]
                sums.append(total)
            return sums

        even_taps, odd_taps = taps[past::-2], taps[past - 1 :: -2]
        odd = window[0::2]
        even = window[1::2]
        evens = convolve(even_taps, even)
        odds = convolve(odd_taps, odd)
        both_taps = [one + two for one, two in zip(even_taps, odd_taps)]
        both = convolve(both_taps, [one + two for one, two in zip(even, odd[1:])])
        for j in range(frame_block // 2):
            pair = (evens[j] + odds[j], both[j] - evens[j] - odds[j + 1])
            for frame, total in zip((2 * j, 2 * j + 1), pair):
                filtered[part, pl.ds(frame, octet, stride=frame_block), :] = total

    kept = pl.ds(pl.multiple_of(step * frame_block, frame_block), frame_block)

    @pl.loop(0, octet)
    def _(antenna):
        for half in range(frame_block // octet):
            rows = pl.ds(pl.multiple_of(antenna * frame_block + half * octet, octet), octet)
            bins = real_transform([filtered[part, rows, :] for part in range(radix)])
            here = pl.ds(half * octet, octet)
            sections[0, here, :] = bins[0][0]
            sections[1, here, :] = bins[radix // 2][0]
            for k in range(1, radix // 2):
                sections[2 * k, here, :] = bins[k][0]
                sections[2 * k + 1, here, :] = bins[k][1]
        for group in range(radix // 2):
            for side in range(2):
                first, second = split_two(sections[2 * group + side])
                high[group, antenna, kept, side * lanes : (side + 1) * lanes] = first
                low[group, antenna, kept, side * lanes : (side + 1) * lanes] = second


def second_stage(high, low, wave_high, wave_low):
    dot = functools.partial(jnp.dot, preferred_element_type=f32)
    return dot(high, wave_high) + (dot(low, wave_high) + dot(high, wave_low))


def divisor(*sizes, most=3):
    return max(n for n in range(1, most + 1) if all(size % n == 0 for size in sizes))


def swap(one, two, width):
    lane = lax.broadcasted_iota(jnp.int32, (1, lanes), 1)
    even = lax.rem(lane // width, 2) == 0
    return (
        jnp.where(even, one, pltpu.roll(two, width, 1)),
        jnp.where(even, pltpu.roll(one, lanes - width, 1), two),
    )


def head_kernel(length, steps, each, size, skipped, *refs):
    before_ref, block_ref, taps_ref, wave_high_ref, wave_low_ref = refs[:5]
    out_ref, *refs = refs[5:]
    filtered, sections, history, turned, high, low, wave_high, wave_low, done = refs
    step = pl.program_id(0)
    frames = high.shape[2]
    radix = length // lanes
    kept = lanes // 2
    taken = pl.ds(2 * skipped, 2 * size)
    waves = [
        pltpu.make_async_copy(wave_high_ref.at[taken], wave_high, done.at[0]),
        pltpu.make_async_copy(wave_low_ref.at[taken], wave_low, done.at[1]),
    ]

    @pl.when(step == 0)
    def _():
        for copy in waves:
            copy.start()
        if steps > 1:
            past = history.shape[1]

            @pl.loop(0, radix, unroll=4)
            def _(part):
                for j in range(past):
                    place = part * lanes + (frame_block - past + j) * length
                    place = pl.ds(pl.multiple_of(place, lanes), lanes)
                    history[part, j] = before_ref[:, place].astype(f32)

    @pl.when(step < steps)
    def _():
        filter_frames(
            length,
            step,
            before_ref,
            block_ref,
            taps_ref,
            high,
            low,
            filtered,
            sections,
            history if steps > 1 else None,
        )

    @pl.when(step == steps)
    def _():
        for copy in waves:
            copy.wait()

    @pl.when(step >= steps)
    def _():
        rows = (octet * frames, 2 * lanes)
        totals = []
        for j in range(2 * each):
            at = (step - steps) * 2 * each + j
            pair = high[2 * skipped + at].reshape(rows), low[2 * skipped + at].reshape(rows)
            totals.append(second_stage(*pair, wave_high[at], wave_low[at]))
        for j in range(each):
            for block in range(steps):
                for a in range(0, octet, 2):
                    piece = []
                    for at in (a, a + 1):
                        begin = at * frames + block * frame_block
                        for total in totals[2 * j : 2 * j + 2]:
                            part = total[begin : begin + frame_block]
                            piece += [part[:, :lanes], part[:, lanes:]]
                    piece = jnp.concatenate(piece, axis=0).T
                    one, two = swap(piece[:kept], piece[kept:], kept)
                    turned[j * steps + block, pl.ds(a, kept, stride=octet), :] = one
                    turned[j * steps + block, pl.ds(a + 1, kept, stride=octet), :] = two
        for j in range(each * steps):
            out_ref[:, j] = turned[j].reshape(kept, octet, lanes).astype(bf16)


def head(before, before_block, samples, taps, tables, first, steps, skipped, size):
    length = taps.shape[1]
    radix = length // lanes
    groups = radix // 2
    kept = lanes // 2
    frames = steps * frame_block
    width = frame_block * length
    each = divisor(size, skipped, most=8 if steps == 1 else 2)
    anywhere = pl.BlockSpec(memory_space=pl.ANY)
    return pl.pallas_call(
        functools.partial(head_kernel, length, steps, each, size, skipped),
        grid=(steps + size // each,),
        in_specs=[
            pl.BlockSpec((octet, width), lambda i: (0, before_block)),
            pl.BlockSpec((octet, width), lambda i: (0, first + jnp.minimum(i, steps - 1))),
            pl.BlockSpec(taps.shape, lambda i: (0, 0)),
            anywhere,
            anywhere,
        ],
        out_specs=pl.BlockSpec(
            (kept, each * steps, octet, lanes), lambda i: (0, jnp.maximum(i - steps, 0), 0, 0)
        ),
        out_shape=jax.ShapeDtypeStruct((kept, size * steps, octet, lanes), bf16),
        scratch_shapes=[
            pltpu.VMEM((radix, frame_block * octet, lanes), f32),
            pltpu.VMEM((radix, frame_block, lanes), f32),
            pltpu.VMEM((radix, taps.shape[0] - 1, octet, lanes), f32),
            pltpu.VMEM((each * steps, kept * octet, lanes), f32),
            pltpu.VMEM((groups, octet, frames, 2 * lanes), bf16),
            pltpu.VMEM((groups, octet, frames, 2 * lanes), bf16),
            pltpu.VMEM((2 * size, 2 * lanes, 2 * lanes), bf16),
            pltpu.VMEM((2 * size, 2 * lanes, 2 * lanes), bf16),
            pltpu.SemaphoreType.DMA((2,)),
        ],
        compiler_params=pltpu.CompilerParams(vmem_limit_bytes=later_vmem if skipped else head_vmem),
        cost_estimate=pl.CostEstimate(
            flops=steps * 1_000_000_000, bytes_accessed=steps * 1_000_000, transcendentals=0
        ),
        name="head",
    )(before, samples, taps, *tables)


def phase_tables(length):
    radix = length // lanes
    kept = lanes // 2
    q = np.arange(lanes)
    m = np.arange(kept)

    def waves(k):
        angle = 2 * np.pi * (np.outer(q, k + radix * m) % length) / length
        return np.cos(angle), np.sin(angle)

    zero = np.zeros((lanes, kept))
    (c, s), (oc, os) = waves(0), waves(radix // 2)
    tables = [np.block([[c, zero, -s, zero], [zero, oc, zero, -os]])]
    for k in range(1, radix // 2):
        (c, s), (oc, os) = waves(k), waves(radix - k)
        tables.append(np.block([[c, oc, -s, -os], [s, -os, c, -oc]]))
    tables = np.stack(tables).astype(np.float32)
    high = tables.astype(ml_dtypes.bfloat16)
    low = (tables - high.astype(np.float32)).astype(ml_dtypes.bfloat16)
    return high, low


def contract_last(left, right):
    return lax.dot_general(left, right, (((1,), (1,)), ((), ())), preferred_element_type=f32)


def covariance_kernel(place, scale, widths, *refs):
    x_refs, q_ref = refs[: len(widths)], refs[len(widths)]
    packed = len(widths) > 1
    out_ref, ready, done = refs[-3:]
    step = pl.program_id(0)
    steps = pl.num_programs(0)
    slot = lax.rem(step, 2)
    octets, shards, runs = x_refs[0].shape[:3]
    antennas = octets * octet
    columns = x_refs[0].shape[3] // widths[0]
    held = [
        (run, j, c) for run in range(runs) for j in range(columns) for c in range(4 if packed else 1)
    ]
    count = len(held)

    def target(at, index):
        run, j, c = held[index]
        return place(run, at * columns + j, c)

    def copies(at, which):
        return [
            pltpu.make_async_copy(
                ready.at[which, j], out_ref.at[target(at, j)], done.at[which, j]
            )
            for j in range(count)
        ]

    @pl.when(step >= 2)
    def _():
        for copy in copies(step - 2, slot):
            copy.wait()

    def load(ref, t, run, j):
        if t >= shards:
            return jnp.zeros((antennas, lanes), f32)
        return ref[:, t, run, j].astype(f32).reshape(antennas, lanes)

    def channels(run, j):
        parts = [[] for _ in range(8 if packed else 2)]
        for t in range(0, shards, 2):
            tiles = [
                load(ref, u, run, j * width + at)
                for u in (t, t + 1)
                for ref, width in zip(x_refs, widths)
                for at in range(width)
            ]
            stride = len(tiles) // 2
            while stride:
                for low in range(len(tiles)):
                    if not low & stride:
                        tiles[low], tiles[low + stride] = swap(
                            tiles[low], tiles[low + stride], lanes * stride // len(tiles)
                        )
                stride //= 2
            for part, tile in zip(parts, tiles):
                part.append(tile)
        return [
            jnp.concatenate(real + imag, axis=1) for real, imag in zip(parts[0::2], parts[1::2])
        ]

    def turned(v):
        middle = v.shape[1] // 2
        return jnp.concatenate([v[:, middle:], -v[:, :middle]], axis=1)

    xs = [x for run in range(runs) for j in range(columns) for x in channels(run, j)]
    qs = [split_three(q_ref[target(step, at)]) for at in range(count)]
    zs = []
    for x, (qh, qm, ql) in zip(xs, qs):
        left = jnp.concatenate([qh, qm, ql, jnp.zeros_like(qh)], axis=0).astype(bf16)
        z = jnp.dot(left, x.astype(bf16), preferred_element_type=f32)
        zs.append(split_three(z[:octet] + z[octet : 2 * octet] + z[2 * octet : 3 * octet]))
    parts = []
    for x, (qh, qm, ql), (zh, zm, zl) in zip(xs, qs, zs):
        left = jnp.concatenate([qh, qh, qm, qm, qh, ql], axis=0).astype(bf16)
        right = jnp.concatenate([zh, zm, zh, zm, zl, zh], axis=0).astype(bf16)
        taken = lax.dot_general(left, right, (((0,), (0,)), ((), ())), preferred_element_type=f32)
        parts.append(split_two(x - taken))
    for at, ((high, low), copy) in enumerate(zip(parts, copies(step, slot))):
        left = jnp.concatenate([high, turned(high)], axis=0)
        total = contract_last(left, jnp.concatenate([high, low], axis=0))
        same, cross = total[:, :antennas], total[:, antennas:]
        real, imag = cross[:antennas], cross[antennas:]
        cross = jnp.concatenate([real + real.T, imag - imag.T], axis=0)
        total = (same + cross) * scale
        ready[slot, at] = total.reshape(2, antennas, antennas)
        copy.start()

    @pl.when(step == steps - 1)
    def _():
        @pl.when(step >= 1)
        def _():
            for copy in copies(step - 1, 1 - slot):
                copy.wait()

        for copy in copies(step, slot):
            copy.wait()


def covariances(received, basis, place, frame_total, total, previous, last):
    array, runs, _, taken, _ = received[0]
    octets, shards = array.shape[:2]
    antennas = octets * octet
    widths = [one[4] for one in received]
    packed = len(received) > 1
    sizes = [begin for _, _, begin, _, _ in received]
    each = divisor(taken, *sizes, most=max(1, 4 // runs) if packed else 8)
    count = runs * each * (4 if packed else 1)
    steps = taken // each

    def window(begin, width):
        return pl.BlockSpec(
            (octets, shards, runs, each * width, octet, lanes),
            lambda i: (0, 0, 0, begin // each + i, 0, 0),
        )

    in_specs = [window(begin, width) for _, _, begin, _, width in received]
    in_specs.append(pl.BlockSpec(basis.shape, lambda i: (0, 0, 0)))
    operands = [one[0].reshape(octets, shards, runs, -1, octet, lanes) for one in received]
    operands.append(basis)
    aliases = {}
    if previous is not None:
        in_specs.append(pl.BlockSpec(memory_space=pl.ANY))
        aliases = {len(operands): 0}
        operands.append(previous)
    return pl.pallas_call(
        functools.partial(covariance_kernel, place, 1.0 / frame_total, widths),
        grid=(steps,),
        in_specs=in_specs,
        out_specs=pl.BlockSpec(memory_space=pl.ANY),
        out_shape=jax.ShapeDtypeStruct((total, 2, antennas, antennas), f32),
        scratch_shapes=[
            pltpu.VMEM((2, count, 2, antennas, antennas), f32),
            pltpu.SemaphoreType.DMA((2, count)),
        ],
        input_output_aliases=aliases,
        compiler_params=pltpu.CompilerParams(vmem_limit_bytes=last_vmem if last else covariance_vmem),
        cost_estimate=pl.CostEstimate(
            flops=steps * count * 200_000_000,
            bytes_accessed=steps * count * 200_000,
            transcendentals=0,
        ),
        name="covariances",
    )(*operands)


def orthonormal(vectors):
    found = []
    for column in range(vectors.shape[1]):
        residue = vectors[:, column, :]
        for earlier in found:
            residue = residue - earlier * jnp.sum(earlier * residue, axis=-1, keepdims=True)
        found.append(
            residue / jnp.sqrt(jnp.sum(residue * residue, axis=-1, keepdims=True) + epsilon)
        )
    return jnp.stack(found, axis=1)


def basis_of(chosen, counted, steering):
    count, slots = chosen.shape
    directions = steering.shape[0]
    onehot = (
        chosen[:, :, None] == lax.broadcasted_iota(jnp.int32, (count, slots, directions), 2)
    ).astype(f32)
    live = (lax.broadcasted_iota(jnp.int32, (count, slots), 1) < counted[:, None]).astype(f32)
    vectors = jnp.einsum("crn,na->cra", onehot, steering, precision=highest) * live[:, :, None]
    basis = orthonormal(vectors)
    return jnp.pad(basis, ((0, 0), (0, octet - slots), (0, 0)))


def per_device(samples, taps, steering, interferer_ids, ranks):
    antennas, width = samples.shape
    length = taps.shape[1]
    frames = width // length
    radix = length // lanes
    groups = radix // 2
    kept = lanes // 2
    shards = lax.axis_size("tm")
    spread = lax.axis_size("chan")
    devices = spread * shards
    owned = interferer_ids.shape[0]
    frame_total = frames * shards

    padded = samples
    if antennas < octet:
        padded = jnp.pad(samples, ((0, octet - antennas), (0, 0)))
    tables = [jnp.asarray(table) for table in phase_tables(length)]
    blocks = frames // frame_block
    whole_runs = owned % radix == 0
    runs = owned // radix
    twos = groups // 2
    cuts = (twos - last_twos, last_twos) if whole_runs else (twos,)

    def exchange(spectra):
        received = lax.all_to_all(spectra, ("chan", "tm"), split_axis=0, concat_axis=0, tiled=True)
        received = received.reshape(spread, shards, -1, antennas, lanes)
        if antennas < octet:
            received = received.transpose(1, 2, 0, 3, 4).reshape(
                shards, -1, spread * antennas // octet, octet, lanes
            ).transpose(2, 0, 1, 3, 4)
        return received

    def channel_at(first):
        def place(run, column, c):
            group = 2 * (first + column) + c % 2
            mirrored = jnp.where(group == 0, groups, radix - group)
            return run * radix + (group if c < 2 else mirrored)

        return place

    early = head(padded, blocks - 2, padded, taps, tables, blocks - 1, 1, 0, twos)
    early, behind = lax.optimization_barrier((early, padded))
    edge = behind[:, width - frame_block * length :]
    before = lax.ppermute(edge, "tm", [(i, i + 1) for i in range(shards - 1)])
    if whole_runs:
        arrived = exchange(early.reshape(devices, -1, octet, lanes))
    basis = basis_of(interferer_ids, ranks, steering)

    def later(first, count):
        return head(before, 0, padded, taps, tables, 0, blocks - 1, first, count)

    out = None
    if whole_runs:
        first = 0
        pieces = []
        for count in cuts:
            if first:
                before, basis = lax.optimization_barrier((before, basis))
            sent = later(first, count).reshape(devices, -1, octet, lanes)
            if not first:
                sent, arrived = lax.optimization_barrier((sent, arrived))
            pieces.append((exchange(sent), first, count))
            first += count
        for received, first, count in pieces:
            parts = (
                (received, runs, 0, count, blocks - 1),
                (arrived, runs, first, count, 1),
            )
            out = covariances(
                parts, basis, channel_at(first), frame_total, owned, out, first > 0
            )
    else:
        tiles = jnp.concatenate(
            [
                later(0, twos).reshape(kept, twos, blocks - 1, octet, 4, 2, frame_block),
                early.reshape(kept, twos, 1, octet, 4, 2, frame_block),
            ],
            axis=2,
        )
        tiles = tiles.transpose(0, 1, 4, 3, 5, 2, 6).reshape(kept, radix, octet, lanes)
        order = [
            k
            for g in range(0, groups, 2)
            for k in (g, g + 1, radix - g if g else groups, radix - g - 1)
        ]
        tiles = tiles[:, np.argsort(order), :antennas].reshape(devices, owned, antennas, lanes)
        received = exchange(tiles)
        parts = ((received, 1, 0, owned, 1),)
        out = covariances(parts, basis, lambda run, column, c: column, frame_total, owned, None, True)
    return out


last_twos = 2
head_vmem = 56 * 1024 * 1024
later_vmem = 32 * 1024 * 1024
covariance_vmem = 24 * 1024 * 1024
last_vmem = 24 * 1024 * 1024


def solution(mesh):
    in_specs = (P("chan", "tm"), P(), P(), P(("chan", "tm"), None), P(("chan", "tm")))
    out_specs = P(("chan", "tm"), None, None, None)
    return jax.shard_map(
        per_device, mesh=mesh, in_specs=in_specs, out_specs=out_specs, check_vma=False
    )
```
